32 devices in a mesh: ang: 8 (over y, x, core), row: 4 (over z).
Axes of the slice: x: 2, y: 2, z: 4, core: 2. Of those that a mesh axis runs over, the one named last changes fastest.
Arguments:
- dual_field: bfloat16 [32, 8, 2048], P('ang', 'row'), may hold values from -2 to 3
- forward: bfloat16 [32, 8, 2048], P('ang', 'row'), may hold values from -2 to 3
- sinogram: bfloat16 [32, 8, 2048], P('ang', 'row'), may hold values from -2 to 3
- first_weight: bfloat16 [3, 3, 32, 3], replicated, may hold values from -1.25 to 1.25
- first_bias: float32 [32], replicated, may hold values from -3 to 3
- middle_weight: bfloat16 [3, 3, 32, 32], replicated, may hold values from -0.375 to 0.375
- middle_bias: float32 [32], replicated, may hold values from -3 to 3
- last_weight: bfloat16 [3, 3, 1, 32], replicated, may hold values from -0.1875 to 0.1875
- magnify: float32 [32], P('ang'), may hold values from 0.85 to 0.95
- detector_shift: float32 [32], P('ang'), may hold values from -8 to 8
- row_fraction: float32 [32], P('ang'), may hold values from 0 to 1
- offsets: int32 [8, 16], replicated, may hold values from 0 to 3, as said below
- slab_order: int32 [16], replicated, may hold values from 0 to 15, each once
Outputs:
- new_dual: bfloat16 [32, 8, 2048], P('ang', 'row')
- volume: float32 [64, 2048], P('row', 'ang')
The draws below stay inside these ranges and needn't reach their ends.
Inputs may be any that keep to these rules, and one draw needn't show every extreme that they name: offsets[b, q] lies within 2 rows of q * 3 // 15. `slab_order`: each slab appears once.
All inputs are finite; a program needn't handle non-finite values.
Results may differ from the reference program's by a relative error of at most 0.0022.
The reference program's roundings to bfloat16 on the way count: a program that leaves them out, or rounds other values in their place, can miss the bound.
Values may be sent and summed in bfloat16 or wider, within the bound.
A program may use at most 64 MiB of HBM per device.

```python
import math
import jax
import jax.numpy as jnp
from jax import lax

ANG_DEV = 4
ROWS_DEV = 2
U = 2048
CH = 32
SLAB_Z = 4
ANGLES = 32
R = 8
SLABS = 16
BLOCKS = 8


def profile_field(key, salt):
    folded = jax.random.fold_in(key, salt)
    noise_key, amp_key, shift_key = jax.random.split(folded, 3)
    noise = jnp.clip(0.6 * jax.random.normal(noise_key, (ANGLES, R, U), jnp.float32), -2.0, 2.0)
    amplitude = jax.random.uniform(amp_key, (ANGLES, R, 1), jnp.float32, 0.6, 1.0)
    shift = jax.random.uniform(shift_key, (ANGLES, 1, 1), jnp.float32, -U / 32.0, U / 32.0)
    columns = jnp.arange(U, dtype=jnp.float32)[None, None, :]
    ratio = (columns - (U - 1) / 2.0 - shift) / (U / 4.0)
    profile = amplitude * jnp.sqrt(jnp.maximum(1.0 - ratio * ratio, 0.0))
    return (noise + profile).astype(jnp.bfloat16)


def draw_dual_field(key, part):
    return profile_field(key, 101)


def draw_forward(key, part):
    return profile_field(key, 202)


def draw_sinogram(key, part):
    return profile_field(key, 303)


def draw_offsets(key, part):
    base_rows = jnp.arange(SLABS, dtype=jnp.int32) * (R - SLAB_Z - 1) // (SLABS - 1)
    jitter = jax.random.randint(key, (BLOCKS, SLABS), -ROWS_DEV, ROWS_DEV + 1)
    return jnp.clip(base_rows[None, :] + jitter, 0, R - SLAB_Z - 1).astype(jnp.int32)


def block_levels(stream_key, dims, cuts, least, high):
    level, own = 1.0, jax.random.fold_in(stream_key, 6)
    for axis_at, blocks in cuts:
        draws = jnp.exp(jax.random.uniform(jax.random.fold_in(own, axis_at), (blocks,), jnp.float32, least / len(cuts), high / len(cuts)))
        level = level * jnp.repeat(draws, dims[axis_at] // blocks).reshape([-1 if axis == axis_at else 1 for axis in range(len(dims))])
    return level


def bell_draw(rng, extent, scale, bound, kind=jnp.bfloat16):
    array = scale * jax.random.normal(rng, extent, jnp.float32)
    return jnp.clip(array, min=-bound, max=bound).astype(kind)


def setup_inputs(seed: int = 0) -> dict:
    seeds = jax.random.split(jax.random.key(seed), 14)
    dual_field = draw_dual_field(jax.random.fold_in(seeds[13], 71), 0)
    forward = draw_forward(jax.random.fold_in(seeds[13], 71), 0)
    sinogram = draw_sinogram(jax.random.fold_in(seeds[13], 71), 0)
    first_weight = bell_draw(seeds[3], (3, 3, CH, 3), 27 ** -0.5, 1.25)
    first_bias = bell_draw(seeds[4], (CH,), 0.5, 3.0, jnp.float32)
    middle_weight = bell_draw(seeds[5], (3, 3, CH, CH), (9 * CH) ** -0.5, 0.375)
    middle_bias = bell_draw(seeds[6], (CH,), 0.5, 3.0, jnp.float32)
    last_weight = bell_draw(seeds[7], (3, 3, 1, CH), (36 * CH) ** -0.5, 0.1875)
    magnify = jnp.clip(0.85 + 0.099999964 * jax.random.uniform(seeds[8], (ANGLES,), jnp.float32) ** block_levels(seeds[8], (ANGLES,), ((0, 8),), -0.2, 0.2), 0.85, 0.95)
    detector_shift = jnp.clip(jax.random.uniform(seeds[9], (ANGLES,), jnp.float32, -8.0, 8.0) * block_levels(seeds[9], (ANGLES,), ((0, 8),), -0.4, 0.0), -8.0, 8.0)
    row_fraction = jnp.clip(1.0 * jax.random.uniform(seeds[10], (ANGLES,), jnp.float32) ** block_levels(seeds[10], (ANGLES,), ((0, 8),), -0.2, 0.2), 0.0, 1.0)
    offsets = draw_offsets(jax.random.fold_in(seeds[13], 71), 0)
    slab_order = jax.random.permutation(seeds[12], SLABS).astype(jnp.int32)
    return {"dual_field": dual_field, "forward": forward, "sinogram": sinogram, "first_weight": first_weight, "first_bias": first_bias, "middle_weight": middle_weight, "middle_bias": middle_bias, "last_weight": last_weight, "magnify": magnify, "detector_shift": detector_shift, "row_fraction": row_fraction, "offsets": offsets, "slab_order": slab_order}


def ramp_block(start, width, size):
    row_ids = jnp.arange(size, dtype=jnp.int32)[:, None]
    col_ids = start + jnp.arange(width, dtype=jnp.int32)[None, :]
    offset_odd = jnp.abs(row_ids - col_ids) % 2 == 1
    distance = jnp.where(offset_odd, row_ids - col_ids, 1).astype(jnp.float32)
    kernel = jnp.where(row_ids == col_ids, 0.25, jnp.where(offset_odd, -1.0 / (math.pi * math.pi * distance * distance), 0.0))
    return kernel.astype(jnp.bfloat16)

def conv_taps(inputs, weights):
    length = inputs.shape[1] - 2
    columns = inputs.shape[2]
    padded = jnp.pad(inputs.astype(jnp.float32), ((0, 0), (0, 0), (1, 1)))
    result = jnp.zeros((weights.shape[2], length, columns), jnp.float32)
    for ang_tap in range(3):
        for col_tap in range(3):
            result = result + jnp.einsum('oc,cau->oau', weights[ang_tap, col_tap].astype(jnp.float32), padded[:, ang_tap:ang_tap + length, col_tap:col_tap + columns])
    return result

def wrap_angles(values):
    return jnp.concatenate([values[:, -1:], values, values[:, :1]], axis=1)

def interpolate(filtered, magnify, detector_shift):
    columns = filtered.shape[2]
    centre = (columns - 1) / 2.0
    places = (jnp.arange(columns, dtype=jnp.float32)[None, :] - centre) * magnify[:, None] + centre + detector_shift[:, None]
    floors = jnp.floor(places)
    weight = (places - floors)[:, None, :]
    low_index = jnp.broadcast_to(floors.astype(jnp.int32)[:, None, :], filtered.shape)
    left_vals = jnp.take_along_axis(filtered, low_index, axis=2)
    right_vals = jnp.take_along_axis(filtered, low_index + 1, axis=2)
    return ((1.0 - weight) * left_vals + weight * right_vals).astype(jnp.bfloat16)

def reference(dual_field, forward, sinogram, first_weight, first_bias, middle_weight, middle_bias, last_weight, magnify, detector_shift, row_fraction, offsets, slab_order):
    stacked = jnp.stack([dual_field, forward, sinogram], axis=0).transpose(2, 0, 1, 3)

    def row_update(row_data):
        first_act = jax.nn.silu(conv_taps(wrap_angles(row_data), first_weight) + first_bias[:, None, None]).astype(jnp.bfloat16)
        second_act = jax.nn.silu(conv_taps(wrap_angles(first_act), middle_weight) + middle_bias[:, None, None]).astype(jnp.bfloat16)
        return conv_taps(wrap_angles(second_act), last_weight)[0]
    update = lax.map(row_update, stacked)
    new_dual = (dual_field.astype(jnp.float32) + update.transpose(1, 0, 2)).astype(jnp.bfloat16)
    filtered = jnp.dot(new_dual.reshape(ANGLES * R, U), ramp_block(0, U, U), preferred_element_type=jnp.float32).reshape(ANGLES, R, U)
    projected = interpolate(filtered, magnify, detector_shift)

    def per_block(running, block_id):
        block_rows = lax.dynamic_slice_in_dim(projected, block_id * ANG_DEV, ANG_DEV, 0)
        fraction = lax.dynamic_slice_in_dim(row_fraction, block_id * ANG_DEV, ANG_DEV, 0).astype(jnp.float32)[:, None, None]
        starts = offsets[block_id][slab_order]
        first_rows = (starts[:, None] + jnp.arange(SLAB_Z, dtype=jnp.int32)[None, :]).reshape(-1)
        lower_rows = jnp.take(block_rows, first_rows, axis=1).astype(jnp.float32)
        upper_rows = jnp.take(block_rows, first_rows + 1, axis=1).astype(jnp.float32)
        return (running + lax.optimization_barrier(jnp.sum((1.0 - fraction) * lower_rows + fraction * upper_rows, axis=0)), None)
    summed, _ = lax.scan(per_block, jnp.zeros((SLABS * SLAB_Z, U), jnp.float32), jnp.arange(BLOCKS, dtype=jnp.int32))
    volume = summed / math.sqrt(ANGLES)
    return (new_dual, volume)
```

```python
import functools
import math

import jax
import jax.numpy as jnp
from jax import lax
from jax.experimental import pallas as pl
from jax.experimental.pallas import tpu as pltpu
from jax.sharding import PartitionSpec as P

SLAB_Z = 4
MAG_LOW, MAG_HIGH, SHIFT_MAX = 0.85, 0.95, 8.0
PAD = 128
TILE = 256
F32 = jnp.float32
BF16 = jnp.bfloat16
MESH = pl.DeviceIdType.MESH


def dot(a, b):
    return jnp.dot(a, b, preferred_element_type=F32)


def silu(v):
    half = 0.5 * v
    return half + half * jnp.tanh(half)


def iota(shape, dim):
    return lax.broadcasted_iota(jnp.int32, shape, dim)


def as_column(row):
    size = row.shape[1]
    spread = jnp.broadcast_to(row, (size, size))
    return jnp.sum(
        jnp.where(iota((size, size), 0) == iota((size, size), 1), spread, 0.0), axis=1, keepdims=True
    )


def by_row(ref, shape, period):
    index = iota(shape, 0) // 2
    value = jnp.full(shape, ref[0], F32)
    for a in range(1, period):
        value = jnp.where(index == a, ref[a], value)
    return value


def shifted(window, width):
    size = window.shape[1]
    left = pltpu.roll(window, 1, 1)[:, PAD : PAD + width]
    right = pltpu.roll(window, size - 1, 1)[:, PAD : PAD + width]
    mid = window[:, PAD : PAD + width]
    return jnp.concatenate([left.astype(BF16), mid.astype(BF16), right.astype(BF16)], axis=0)


def kernel(
    n_ang, n_row, dual, forward, sino, fw, fb, mw, mb, lw, mag, shift, frac, offsets, order,
    nd_out, vol_out,
    halo, x1, x2, x3, taps, w1, w2, w3, ramp, frac_own, frac_all, sent, got,
    halo_send, halo_recv, frac_send, frac_recv, send_sem, recv_sem,
):
    angs, rows, cols = dual.shape
    ch = fw.shape[2]
    total = n_ang * n_row
    my_ang, my_row = lax.axis_index("ang"), lax.axis_index("row")
    me = my_ang * n_row + my_row
    wide = angs + 6
    out1, out2 = angs + 4, angs + 2
    ar = angs * rows
    per = 64

    def place_of(step):
        target = lax.rem(me + step, total)
        return target, target // n_row, lax.rem(target, n_row)

    barrier = pltpu.get_barrier_semaphore()

    def greet(step, carry):
        _, ang, row = place_of(step)
        pl.semaphore_signal(barrier, inc=1, device_id=(ang, row), device_id_type=MESH)
        return carry

    lax.fori_loop(1, total, greet, 0)

    lane = iota((8, 128), 1)
    mine = jnp.full((8, 128), frac[0], F32)
    for a in range(1, angs):
        mine = jnp.where((lane // rows) % angs == a, frac[a], mine)
    frac_own[...] = mine
    frac_all[my_ang] = mine
    pl.semaphore_wait(barrier, total - 1)

    left = lax.rem(my_ang + n_ang - 1, n_ang)
    right = lax.rem(my_ang + 1, n_ang)
    halo_copies = []
    for c, ref in enumerate((dual, forward, sino)):
        for side, (peer, first) in enumerate(((right, angs - 3), (left, 0))):
            copy = pltpu.make_async_remote_copy(
                src_ref=ref.at[pl.ds(first, 3)],
                dst_ref=halo.at[side, c],
                send_sem=halo_send.at[side, c],
                recv_sem=halo_recv.at[side, c],
                device_id=(peer, my_row),
                device_id_type=MESH,
            )
            copy.start()
            halo_copies.append(copy)

    def frac_copy(source, target):
        return pltpu.make_async_remote_copy(
            src_ref=frac_own,
            dst_ref=frac_all.at[source],
            send_sem=frac_send.at[target],
            recv_sem=frac_recv.at[source],
            device_id=(target, my_row),
            device_id_type=MESH,
        )

    def frac_start(step, carry):
        frac_copy(my_ang, lax.rem(my_ang + step, n_ang)).start()
        return carry

    lax.fori_loop(1, n_ang, frac_start, 0)

    k1 = 3 * per
    pick1 = iota((3, k1), 1) % per // (wide * rows) == iota((3, k1), 0)
    pick1 = jnp.where(pick1, 1.0, 0.0).astype(BF16)
    place1 = iota((ch, k1), 1)
    tap1, rest1 = place1 // per, place1 % per
    ang1 = jnp.where(rest1 < 3 * wide * rows, rest1 % (wide * rows) // rows, -9)
    row1 = rest1 % rows
    tiles1 = [[dot(fw[i, j], pick1) for j in range(3)] for i in range(3)]
    joined1 = [
        jnp.where(tap1 == 0, tiles1[i][0], jnp.where(tap1 == 1, tiles1[i][1], tiles1[i][2]))
        for i in range(3)
    ]
    for r in range(rows):
        for a in range(out1):
            block = jnp.zeros((ch, k1), F32)
            for i in range(3):
                block = jnp.where((ang1 == a + i) & (row1 == r), joined1[i], block)
            w1[pl.ds((r * out1 + a) * ch, ch), :] = block.astype(BF16)

    k2 = out1 * ch
    pick2 = jnp.where(iota((ch, k2), 1) % ch == iota((ch, k2), 0), 1.0, 0.0).astype(BF16)
    ang2 = iota((ch, k2), 1) // ch
    for j in range(3):
        tiles2 = [dot(mw[i, j], pick2) for i in range(3)]
        for a in range(out2):
            block = jnp.zeros((ch, k2), F32)
            for i in range(3):
                block = jnp.where(ang2 == a + i, tiles2[i], block)
            w2[pl.ds(a * ch, ch), pl.ds(j * k2, k2)] = block.astype(BF16)

    k3 = rows * out2 * ch
    pick3 = jnp.where(iota((ch, k3), 1) % ch == iota((ch, k3), 0), 1.0, 0.0).astype(BF16)
    place3 = iota((ar, k3), 1)
    ang3 = place3 // ch % out2 - iota((ar, k3), 0) // rows
    same3 = place3 // (out2 * ch) == iota((ar, k3), 0) % rows
    for j in range(3):
        block = jnp.zeros((ar, k3), F32)
        for i in range(3):
            weights = jnp.broadcast_to(lw[i, j].astype(F32), (ar, ch)).astype(BF16)
            block = jnp.where((ang3 == i) & same3, dot(weights, pick3), block)
        w3[pl.ds(j * ar, ar), :] = block

    blocks = cols // TILE

    def ramp_block(b, carry):
        away = (b - (blocks - 1)) * TILE + iota((TILE, TILE), 1) - iota((TILE, TILE), 0)
        odd = away % 2 == 1
        distance = jnp.where(odd, away, 1).astype(F32)
        value = jnp.where(odd, -1.0 / (math.pi * math.pi * distance * distance), 0.0)
        ramp[b] = jnp.where(away == 0, 0.25, value).astype(BF16)
        return carry

    lax.fori_loop(0, 2 * blocks - 1, ramp_block, 0)

    bias1 = jnp.concatenate([as_column(fb[...])] * (rows * out1), axis=0)
    bias2 = jnp.concatenate([as_column(mb[...])] * out2, axis=0)

    x1[...] = jnp.zeros_like(x1)
    x2[:, pl.ds(0, PAD)] = jnp.zeros((x2.shape[0], PAD), F32)
    x2[:, pl.ds(PAD + cols, PAD)] = jnp.zeros((x2.shape[0], PAD), F32)
    for c, ref in enumerate((dual, forward, sino)):
        for a in range(angs):
            x1[pl.ds((c * wide + 3 + a) * rows, rows), pl.ds(PAD, cols)] = ref[a].astype(F32)
    for copy in halo_copies:
        copy.wait()
    for c in range(3):
        for a in range(3):
            x1[pl.ds((c * wide + a) * rows, rows), pl.ds(PAD, cols)] = halo[0, c, a].astype(F32)
            x1[pl.ds((c * wide + 3 + angs + a) * rows, rows), pl.ds(PAD, cols)] = halo[1, c, a].astype(F32)

    def layer1(t, carry):
        start = pl.multiple_of(t * TILE, TILE)
        stack = shifted(x1[:, pl.ds(start, TILE + 2 * PAD)], TILE)
        x2[:, pl.ds(start + PAD, TILE)] = silu(dot(w1[...], stack) + bias1)
        return carry

    lax.fori_loop(0, blocks, layer1, 0)

    def layer2(t, carry):
        start = pl.multiple_of(t * TILE, TILE)
        for r in range(rows):
            stack = shifted(x2[pl.ds(r * k2, k2), pl.ds(start, TILE + 2 * PAD)], TILE)
            value = silu(dot(w2[...], stack) + bias2)
            x3[pl.ds(r * out2 * ch, out2 * ch), :] = value.astype(BF16)
        taps[:, pl.ds(start, TILE)] = dot(w3[...].astype(BF16), x3[...])
        return carry

    lax.fori_loop(0, blocks, layer2, 0)

    column = iota((ar, cols), 1)
    before = jnp.where(column == 0, 0.0, pltpu.roll(taps[0:ar, :], 1, 1))
    after = jnp.where(column == cols - 1, 0.0, pltpu.roll(taps[2 * ar : 3 * ar, :], cols - 1, 1))
    update = before + taps[ar : 2 * ar, :] + after
    own = x1[pl.ds(3 * rows, ar), pl.ds(PAD, cols)]
    new_dual = (own + update).astype(BF16).astype(F32)
    for a in range(angs):
        nd_out[a] = new_dual[a * rows : (a + 1) * rows].astype(BF16)

    pieces = jnp.concatenate(
        [new_dual[:, b * TILE : (b + 1) * TILE] for b in range(blocks)], axis=0
    ).astype(BF16)
    filtered = [None] * blocks
    for b in range(2 * blocks - 1):
        product = dot(pieces, ramp[b])
        for source in range(blocks):
            goal = source + b - (blocks - 1)
            if 0 <= goal < blocks:
                part = product[source * ar : (source + 1) * ar]
                filtered[goal] = part if filtered[goal] is None else filtered[goal] + part
    lanes = [filtered[n // 2][:, n % 2 * 128 : n % 2 * 128 + 128] for n in range(cols // 128)]

    centre = (cols - 1) / 2.0
    mags = by_row(mag, (ar, 128), angs)
    shifts = by_row(shift, (ar, 128), angs)
    projected = []
    for n in range(cols // 128):
        edges = [
            (x - centre) * m + centre + s
            for x in (n * 128, n * 128 + 127)
            for m in (MAG_LOW, MAG_HIGH)
            for s in (-SHIFT_MAX, SHIFT_MAX)
        ]
        lowest = max(int((min(edges) - 0.1) // 128), 0)
        highest = min(int((max(edges) + 1.1) // 128), cols // 128 - 1)
        places = ((iota((ar, 128), 1) + n * 128).astype(F32) - centre) * mags + centre + shifts
        floors = jnp.floor(places)
        weight = places - floors
        low = floors.astype(jnp.int32)
        ends = []
        for index in (low, low + 1):
            value = jnp.zeros((ar, 128), F32)
            for k in range(lowest, highest + 1):
                taken = jnp.take_along_axis(lanes[k], index & 127, axis=1)
                value = jnp.where(index >> 7 == k, taken, value)
            ends.append(value)
        projected.append((1.0 - weight) * ends[0] + weight * ends[1])

    halves = cols // n_ang // 128
    size = halves * ar
    for p in range(n_ang):
        sent[p] = jnp.concatenate(projected[p * halves : (p + 1) * halves], axis=0).astype(BF16)

    def block_copy(source, target, ang, row):
        return pltpu.make_async_remote_copy(
            src_ref=sent.at[ang],
            dst_ref=got.at[source],
            send_sem=send_sem.at[target],
            recv_sem=recv_sem.at[source],
            device_id=(ang, row),
            device_id_type=MESH,
        )

    def block_start(step, carry):
        target, ang, row = place_of(step)
        block_copy(me, target, ang, row).start()
        return carry

    lax.fori_loop(1, total, block_start, 0)
    got[me] = sent[my_ang]

    def frac_wait(step, carry):
        peer = lax.rem(my_ang + step, n_ang)
        frac_copy(peer, peer).wait()
        return carry

    lax.fori_loop(1, n_ang, frac_wait, 0)

    slots = order.shape[0] // n_row
    depth = total * size
    zs = slots * SLAB_Z
    place = iota((zs, depth), 1)
    level = iota((zs, depth), 0)
    source_ang = place // (n_row * size)
    piece_row = place // size % n_row * rows + place % rows
    half_of = place % size // ar
    starts = jnp.zeros((zs, depth), jnp.int32)
    fraction = jnp.zeros((zs, depth), F32)
    for p in range(n_ang):
        here = source_ang == p
        spread = jnp.concatenate([frac_all[p][0:1]] * (depth // 128), axis=1)
        fraction = jnp.where(here, jnp.broadcast_to(spread, (zs, depth)), fraction)
        for k in range(slots):
            first = offsets[p, order[my_row * slots + k]]
            starts = jnp.where(here & (level // SLAB_Z == k), first, starts)
    reach = piece_row - starts - level % SLAB_Z
    weights = jnp.where(reach == 0, 1.0 - fraction, jnp.where(reach == 1, fraction, 0.0))
    parts = []
    for h in range(halves):
        left_over = jnp.where(half_of == h, weights, 0.0)
        for _ in range(3):
            part = left_over.astype(BF16)
            left_over = left_over - part.astype(F32)
            parts.append(part)
    stacked = jnp.concatenate(parts, axis=0)

    def block_wait(step, carry):
        target, ang, row = place_of(step)
        block_copy(target, target, ang, row).wait()
        return carry

    lax.fori_loop(1, total, block_wait, 0)

    sums = dot(stacked, got[...].reshape(depth, 128))
    for h in range(halves):
        three = [sums[(h * 3 + s) * zs : (h * 3 + s + 1) * zs] for s in range(3)]
        vol_out[:, pl.ds(h * 128, 128)] = (three[2] + three[1] + three[0]) / math.sqrt(n_ang * angs)


def per_device(
    n_ang, n_row, dual_field, forward, sinogram, first_weight, first_bias, middle_weight,
    middle_bias, last_weight, magnify, detector_shift, row_fraction, offsets, slab_order,
):
    angs, rows, cols = dual_field.shape
    ch = first_weight.shape[2]
    total = n_ang * n_row
    ar = angs * rows
    out1, out2 = angs + 4, angs + 2
    blocks = cols // TILE
    width = cols // n_ang
    size = width // 128 * ar
    slots = slab_order.shape[0] // n_row
    vmem = pl.BlockSpec(memory_space=pltpu.VMEM)
    smem = pl.BlockSpec(memory_space=pltpu.SMEM)
    dma = pltpu.SemaphoreType.DMA
    return pl.pallas_call(
        functools.partial(kernel, n_ang, n_row),
        out_shape=(
            jax.ShapeDtypeStruct(dual_field.shape, BF16),
            jax.ShapeDtypeStruct((slots * SLAB_Z, width), F32),
        ),
        in_specs=[vmem] * 8 + [smem] * 5,
        out_specs=(vmem, vmem),
        scratch_shapes=[
            pltpu.VMEM((2, 3, 3, rows, cols), BF16),
            pltpu.VMEM((64, cols + 2 * PAD), F32),
            pltpu.VMEM((rows * out1 * ch, cols + 2 * PAD), F32),
            pltpu.VMEM((rows * out2 * ch, TILE), BF16),
            pltpu.VMEM((3 * ar, cols), F32),
            pltpu.VMEM((rows * out1 * ch, 3 * 64), BF16),
            pltpu.VMEM((out2 * ch, 3 * out1 * ch), BF16),
            pltpu.VMEM((3 * ar, rows * out2 * ch), F32),
            pltpu.VMEM((2 * blocks - 1, TILE, TILE), BF16),
            pltpu.VMEM((8, 128), F32),
            pltpu.VMEM((n_ang, 8, 128), F32),
            pltpu.VMEM((n_ang, size, 128), BF16),
            pltpu.VMEM((total, size, 128), BF16),
            dma((2, 3)),
            dma((2, 3)),
            dma((n_ang,)),
            dma((n_ang,)),
            dma((total,)),
            dma((total,)),
        ],
        compiler_params=pltpu.CompilerParams(
            collective_id=0, has_side_effects=True, vmem_limit_bytes=40 * 1024 * 1024
        ),
        cost_estimate=pl.CostEstimate(flops=10**9, bytes_accessed=10**6, transcendentals=0),
    )(
        dual_field, forward, sinogram, first_weight, first_bias[None, :], middle_weight,
        middle_bias[None, :], last_weight, magnify, detector_shift, row_fraction, offsets, slab_order,
    )


def solution(mesh):
    sizes = dict(mesh.shape)
    split = P("ang", "row", None)
    return jax.shard_map(
        functools.partial(per_device, sizes["ang"], sizes["row"]),
        mesh=mesh,
        in_specs=(
            split, split, split, P(), P(), P(), P(), P(), P("ang"), P("ang"), P("ang"), P(), P(),
        ),
        out_specs=(split, P("row", "ang")),
        check_vma=False,
    )
```

```python
import functools
import math

import jax
import jax.numpy as jnp
from jax import lax
from jax.experimental import pallas as pl
from jax.experimental.pallas import tpu as pltpu
from jax.sharding import PartitionSpec as P

SLAB_Z = 4
MAG_LOW, MAG_HIGH, SHIFT_MAX = 0.85, 0.95, 8.0
TILE = 256
F32 = jnp.float32
BF16 = jnp.bfloat16
MESH = pl.DeviceIdType.MESH


def dot(a, b):
    return jnp.dot(a, b, preferred_element_type=F32)


def silu(v):
    half = 0.5 * v
    return half + half * jnp.tanh(half)


def iota(shape, dim):
    return lax.broadcasted_iota(jnp.int32, shape, dim)


def as_column(row):
    size = row.shape[1]
    spread = jnp.broadcast_to(row, (size, size))
    return jnp.sum(
        jnp.where(iota((size, size), 0) == iota((size, size), 1), spread, 0.0), axis=1, keepdims=True
    )


def by_row(ref, shape, period):
    index = iota(shape, 0) // 2
    value = jnp.full(shape, ref[0], F32)
    for a in range(1, period):
        value = jnp.where(index == a, ref[a], value)
    return value


def log2(size):
    assert size & (size - 1) == 0
    return size.bit_length() - 1


def split(value, size, count):
    quotient = jnp.zeros_like(value)
    for k in range(1, count):
        quotient = quotient + jnp.where(value >= k * size, 1, 0)
    return quotient, value - quotient * size


def shifted(values):
    cols = values.shape[1]
    column = iota(values.shape, 1)
    zero = jnp.zeros_like(values)
    before = jnp.where(column == 0, zero, pltpu.roll(values, 1, 1))
    after = jnp.where(column == cols - 1, zero, pltpu.roll(values, cols - 1, 1))
    return before, after


def kernel(
    n_ang, n_row, *refs,
):
    sources, (nd_out, vol_out), locals_ = refs[:13], refs[13:15], refs[15:28]
    dual, forward, sino, fw, fb, mw, mb, lw, mag, shift, frac, offsets, order = locals_
    (
    halo, x1, x1s, x2, x3, taps, w1, w2, w3, ramp, frac_own, frac_all, sent, got,
    halo_send, halo_recv, frac_send, frac_recv, send_sem, recv_sem, local_sem,
    ) = refs[28:]
    loads = [
        pltpu.make_async_copy(source, goal, local_sem.at[n])
        for n, (source, goal) in enumerate(zip(sources, locals_))
    ]
    for load in loads:
        load.start()
    angs, rows, cols = dual.shape
    ch = mw.shape[2]
    total = n_ang * n_row
    my_ang, my_row = lax.axis_index("ang"), lax.axis_index("row")
    me = my_ang * n_row + my_row
    wide = angs + 6
    out1, out2 = angs + 4, angs + 2
    ar = angs * rows
    per = 64

    def place_of(step):
        target = lax.rem(me + step, total)
        return target, target // n_row, lax.rem(target, n_row)

    barrier = pltpu.get_barrier_semaphore()

    def greet(step, carry):
        _, ang, row = place_of(step)
        pl.semaphore_signal(barrier, inc=1, device_id=(ang, row), device_id_type=MESH)
        return carry

    lax.fori_loop(1, total, greet, 0)

    narrow = cols // 128

    def ramp_block(b, carry):
        away = (b - (narrow - 1)) * 128 + iota((128, 128), 1) - iota((128, 128), 0)
        odd = (away & 1) == 1
        distance = jnp.where(odd, away, 1).astype(F32)
        value = jnp.where(odd, -1.0 / (math.pi * math.pi * distance * distance), 0.0)
        ramp[:, pl.ds(pl.multiple_of(b * 128, 128), 128)] = jnp.where(away == 0, 0.25, value).astype(BF16)
        return carry

    lax.fori_loop(0, 2 * narrow - 1, ramp_block, 0)
    pl.semaphore_wait(barrier, total - 1)

    left = lax.rem(my_ang + n_ang - 1, n_ang)
    right = lax.rem(my_ang + 1, n_ang)
    halo_copies = []
    for c, ref in enumerate(sources[:3]):
        for side, (peer, first) in enumerate(((right, angs - 3), (left, 0))):
            copy = pltpu.make_async_remote_copy(
                src_ref=ref.at[pl.ds(first, 3)],
                dst_ref=halo.at[side, c],
                send_sem=halo_send.at[side, c],
                recv_sem=halo_recv.at[side, c],
                device_id=(peer, my_row),
                device_id_type=MESH,
            )
            copy.start()
            halo_copies.append(copy)

    for load in loads:
        load.wait()
    lane = iota((8, 128), 1)
    mine = jnp.full((8, 128), frac[0], F32)
    for a in range(1, angs):
        mine = jnp.where((lane & (ar - 1)) // rows == a, frac[a], mine)
    frac_own[...] = mine
    frac_all[my_ang] = mine

    def frac_copy(source, target):
        return pltpu.make_async_remote_copy(
            src_ref=frac_own,
            dst_ref=frac_all.at[source],
            send_sem=frac_send.at[target],
            recv_sem=frac_recv.at[source],
            device_id=(target, my_row),
            device_id_type=MESH,
        )

    def frac_start(step, carry):
        frac_copy(my_ang, lax.rem(my_ang + step, n_ang)).start()
        return carry

    lax.fori_loop(1, n_ang, frac_start, 0)

    k1 = 3 * per
    tap1, rest1 = split(iota((ch, k1), 1), per, 3)
    chan1, rest1 = split(rest1, wide * rows, 4)
    ang1 = jnp.where(chan1 < 3, rest1 >> 1, -9)
    row1 = rest1 & 1
    pick1 = jnp.where(chan1[0:3] == iota((3, k1), 0), 1.0, 0.0).astype(BF16)
    tiles1 = [
        [
            lax.dot_general(fw[i, j], pick1, (((0,), (0,)), ((), ())), preferred_element_type=F32)
            for j in range(3)
        ]
        for i in range(3)
    ]
    joined1 = [
        jnp.where(tap1 == 0, tiles1[i][0], jnp.where(tap1 == 1, tiles1[i][1], tiles1[i][2]))
        for i in range(3)
    ]
    for r in range(rows):
        for a in range(out1):
            block = jnp.zeros((ch, k1), F32)
            for i in range(3):
                block = jnp.where((ang1 == a + i) & (row1 == r), joined1[i], block)
            w1[pl.ds((r * out1 + a) * ch, ch), :] = block.astype(BF16)

    k2 = out1 * ch
    pick2 = jnp.where((iota((ch, k2), 1) & (ch - 1)) == iota((ch, k2), 0), 1.0, 0.0).astype(BF16)
    ang2, _ = split(iota((ch, k2), 1), ch, out1)
    for j in range(3):
        tiles2 = [dot(mw[i, j], pick2) for i in range(3)]
        for a in range(out2):
            block = jnp.zeros((ch, k2), F32)
            for i in range(3):
                block = jnp.where(ang2 == a + i, tiles2[i], block)
            w2[pl.ds(a * ch, ch), pl.ds(j * k2, k2)] = block.astype(BF16)

    k3 = rows * out2 * ch
    pick3 = jnp.where((iota((ch, k3), 1) & (ch - 1)) == iota((ch, k3), 0), 1.0, 0.0).astype(BF16)
    row3, rest3 = split(iota((ar, k3), 1), out2 * ch, rows)
    ang3, _ = split(rest3, ch, out2)
    ang3 = ang3 - (iota((ar, k3), 0) >> 1)
    same3 = row3 == (iota((ar, k3), 0) & 1)
    blocks3 = []
    for j in range(3):
        block = jnp.zeros((ar, k3), F32)
        for i in range(3):
            weights = jnp.broadcast_to(lw[i, 0, j : j + 1, :].astype(F32), (ar, ch)).astype(BF16)
            block = jnp.where((ang3 == i) & same3, dot(weights, pick3), block)
        blocks3.append(block)
    blocks3.append(jnp.zeros((ar, k3), F32))
    w3[...] = jnp.concatenate(blocks3, axis=0).astype(BF16)

    bias1 = jnp.concatenate([as_column(fb[...])] * (rows * out1), axis=0)
    bias2 = jnp.concatenate([as_column(mb[...])] * out2, axis=0)

    x1[...] = jnp.zeros_like(x1)
    for c, ref in enumerate((dual, forward, sino)):
        for a in range(angs):
            x1[pl.ds((c * wide + 3 + a) * rows, rows), :] = ref[a].astype(F32)
    for copy in halo_copies:
        copy.wait()
    for c in range(3):
        for a in range(3):
            x1[pl.ds((c * wide + a) * rows, rows), :] = halo[0, c, a].astype(F32)
            x1[pl.ds((c * wide + 3 + angs + a) * rows, rows), :] = halo[1, c, a].astype(F32)
    middle = x1[...].astype(BF16)
    before, after = shifted(middle)
    x1s[pl.ds(0, per), :] = before
    x1s[pl.ds(per, per), :] = middle
    x1s[pl.ds(2 * per, per), :] = after
    tiles = cols // TILE

    def layer1(t, carry):
        start = pl.multiple_of(t * TILE, TILE)
        value = silu(dot(w1[...], x1s[:, pl.ds(start, TILE)]) + bias1).astype(BF16)
        for r in range(rows):
            x2[pl.ds((r * 3 + 1) * k2, k2), pl.ds(start, TILE)] = value[r * k2 : (r + 1) * k2]
        return carry

    lax.fori_loop(0, tiles, layer1, 0)

    def shift2(n, carry):
        for r in range(rows):
            base = r * 3 * k2 + n * ch
            values = x2[pl.ds(pl.multiple_of(base + k2, ch), ch), :]
            before, after = shifted(values)
            x2[pl.ds(pl.multiple_of(base, ch), ch), :] = before
            x2[pl.ds(pl.multiple_of(base + 2 * k2, ch), ch), :] = after
        return carry

    lax.fori_loop(0, out1, shift2, 0)

    def layer2(t, carry):
        start = pl.multiple_of(t * TILE, TILE)
        for r in range(rows):
            value = silu(dot(w2[...], x2[pl.ds(r * 3 * k2, 3 * k2), pl.ds(start, TILE)]) + bias2)
            x3[pl.ds(r * out2 * ch, out2 * ch), :] = value.astype(BF16)
        taps[:, pl.ds(start, TILE)] = dot(w3[...], x3[...])[0 : 3 * ar]
        return carry

    lax.fori_loop(0, tiles, layer2, 0)

    column = iota((ar, cols), 1)
    before = jnp.where(column == 0, 0.0, pltpu.roll(taps[0:ar, :], 1, 1))
    after = jnp.where(column == cols - 1, 0.0, pltpu.roll(taps[2 * ar : 3 * ar, :], cols - 1, 1))
    update = before + taps[ar : 2 * ar, :] + after
    own = x1[pl.ds(3 * rows, ar), :]
    new_dual = (own + update).astype(BF16).astype(F32)
    for a in range(angs):
        nd_out[a] = new_dual[a * rows : (a + 1) * rows].astype(BF16)

    pieces = jnp.concatenate(
        [new_dual[:, n * 128 : (n + 1) * 128] for n in range(narrow)], axis=0
    ).astype(BF16)
    lanes = [None] * narrow
    for pair in range(0, 2 * narrow - 1, 2):
        near = min(2, 2 * narrow - 1 - pair)
        product = dot(pieces, ramp[:, pl.ds(pair * 128, near * 128)])
        for b in range(pair, pair + near):
            for source in range(narrow):
                goal = source + b - (narrow - 1)
                if 0 <= goal < narrow:
                    at = (b - pair) * 128
                    part = product[source * ar : (source + 1) * ar, at : at + 128]
                    lanes[goal] = part if lanes[goal] is None else lanes[goal] + part

    centre = (cols - 1) / 2.0
    mags = by_row(mag, (ar, 128), angs)
    shifts = by_row(shift, (ar, 128), angs)
    projected = []
    for n in range(cols // 128):
        edges = [
            (x - centre) * m + centre + s
            for x in (n * 128, n * 128 + 127)
            for m in (MAG_LOW, MAG_HIGH)
            for s in (-SHIFT_MAX, SHIFT_MAX)
        ]
        lowest = max(int((min(edges) - 0.1) // 128), 0)
        highest = min(int((max(edges) + 1.1) // 128), cols // 128 - 1)
        places = ((iota((ar, 128), 1) + n * 128).astype(F32) - centre) * mags + centre + shifts
        floors = jnp.floor(places)
        weight = places - floors
        low = floors.astype(jnp.int32)
        ends = []
        for index in (low, low + 1):
            value = jnp.zeros((ar, 128), F32)
            for k in range(lowest, highest + 1):
                taken = jnp.take_along_axis(lanes[k], index & 127, axis=1)
                value = jnp.where(index >> 7 == k, taken, value)
            ends.append(value)
        projected.append((1.0 - weight) * ends[0] + weight * ends[1])

    halves = cols // n_ang // 128
    size = halves * ar
    for p in range(n_ang):
        sent[p] = jnp.concatenate(projected[p * halves : (p + 1) * halves], axis=0).astype(BF16)

    def block_copy(source, target, ang, row):
        return pltpu.make_async_remote_copy(
            src_ref=sent.at[ang],
            dst_ref=got.at[source],
            send_sem=send_sem.at[target],
            recv_sem=recv_sem.at[source],
            device_id=(ang, row),
            device_id_type=MESH,
        )

    def block_start(step, carry):
        target, ang, row = place_of(step)
        block_copy(me, target, ang, row).start()
        return carry

    lax.fori_loop(1, total, block_start, 0)
    got[me] = sent[my_ang]

    def frac_wait(step, carry):
        peer = lax.rem(my_ang + step, n_ang)
        frac_copy(peer, peer).wait()
        return carry

    lax.fori_loop(1, n_ang, frac_wait, 0)

    slots = order.shape[0] // n_row
    depth = total * size
    zs = slots * SLAB_Z
    place = iota((zs, depth), 1)
    level = iota((zs, depth), 0)
    source_ang = (place >> log2(n_row * size))
    piece_row = ((place >> log2(size)) & (n_row - 1)) * rows + (place & (rows - 1))
    half_of = ((place & (size - 1)) >> log2(ar))
    starts = jnp.zeros((zs, depth), jnp.int32)
    fraction = jnp.zeros((zs, depth), F32)
    for p in range(n_ang):
        here = source_ang == p
        spread = jnp.concatenate([frac_all[p][0:1]] * (depth // 128), axis=1)
        fraction = jnp.where(here, jnp.broadcast_to(spread, (zs, depth)), fraction)
        for k in range(slots):
            first = offsets[p, order[my_row * slots + k]]
            starts = jnp.where(here & ((level >> log2(SLAB_Z)) == k), first, starts)
    reach = piece_row - starts - (level & (SLAB_Z - 1))
    weights = jnp.where(reach == 0, 1.0 - fraction, jnp.where(reach == 1, fraction, 0.0))
    parts = []
    for h in range(halves):
        left_over = jnp.where(half_of == h, weights, 0.0)
        for _ in range(3):
            part = left_over.astype(BF16)
            left_over = left_over - part.astype(F32)
            parts.append(part)
    stacked = jnp.concatenate(parts, axis=0)

    def block_wait(step, carry):
        target, ang, row = place_of(step)
        block_copy(target, target, ang, row).wait()
        return carry

    lax.fori_loop(1, total, block_wait, 0)

    sums = dot(stacked, got[...].reshape(depth, 128))
    for h in range(halves):
        three = [sums[(h * 3 + s) * zs : (h * 3 + s + 1) * zs] for s in range(3)]
        vol_out[:, pl.ds(h * 128, 128)] = (three[2] + three[1] + three[0]) / math.sqrt(n_ang * angs)


def per_device(
    n_ang, n_row, dual_field, forward, sinogram, first_weight, first_bias, middle_weight,
    middle_bias, last_weight, magnify, detector_shift, row_fraction, offsets, slab_order,
):
    angs, rows, cols = dual_field.shape
    ch = first_weight.shape[2]
    operands = (
        dual_field, forward, sinogram, first_weight.transpose(0, 1, 3, 2), first_bias[None, :],
        middle_weight, middle_bias[None, :], last_weight.transpose(0, 2, 1, 3), magnify,
        detector_shift, row_fraction, offsets, slab_order,
    )
    total = n_ang * n_row
    ar = angs * rows
    out1, out2 = angs + 4, angs + 2
    narrow = cols // 128
    width = cols // n_ang
    size = width // 128 * ar
    slots = slab_order.shape[0] // n_row
    vmem = pl.BlockSpec(memory_space=pltpu.VMEM)
    dma = pltpu.SemaphoreType.DMA
    return pl.pallas_call(
        functools.partial(kernel, n_ang, n_row),
        out_shape=(
            jax.ShapeDtypeStruct(dual_field.shape, BF16),
            jax.ShapeDtypeStruct((slots * SLAB_Z, width), F32),
        ),
        in_specs=[pl.BlockSpec(memory_space=pltpu.HBM)] * 13,
        out_specs=(vmem, vmem),
        scratch_shapes=[pltpu.VMEM(x.shape, x.dtype) for x in operands[:8]]
        + [pltpu.SMEM(x.shape, x.dtype) for x in operands[8:]]
        + [
            pltpu.VMEM((2, 3, 3, rows, cols), BF16),
            pltpu.VMEM((64, cols), F32),
            pltpu.VMEM((3 * 64, cols), BF16),
            pltpu.VMEM((rows * 3 * out1 * ch, cols), BF16),
            pltpu.VMEM((rows * out2 * ch, TILE), BF16),
            pltpu.VMEM((3 * ar, cols), F32),
            pltpu.VMEM((rows * out1 * ch, 3 * 64), BF16),
            pltpu.VMEM((out2 * ch, 3 * out1 * ch), BF16),
            pltpu.VMEM((4 * ar, rows * out2 * ch), BF16),
            pltpu.VMEM((128, (2 * narrow - 1) * 128), BF16),
            pltpu.VMEM((8, 128), F32),
            pltpu.VMEM((n_ang, 8, 128), F32),
            pltpu.VMEM((n_ang, size, 128), BF16),
            pltpu.VMEM((total, size, 128), BF16),
            dma((2, 3)),
            dma((2, 3)),
            dma((n_ang,)),
            dma((n_ang,)),
            dma((total,)),
            dma((total,)),
            dma((13,)),
        ],
        compiler_params=pltpu.CompilerParams(
            collective_id=0, has_side_effects=True, vmem_limit_bytes=65280 * 1024
        ),
        cost_estimate=pl.CostEstimate(flops=10**9, bytes_accessed=10**6, transcendentals=0),
    )(*operands)


def solution(mesh):
    sizes = dict(mesh.shape)
    split = P("ang", "row", None)
    return jax.shard_map(
        functools.partial(per_device, sizes["ang"], sizes["row"]),
        mesh=mesh,
        in_specs=(
            split, split, split, P(), P(), P(), P(), P(), P("ang"), P("ang"), P("ang"), P(), P(),
        ),
        out_specs=(split, P("row", "ang")),
        check_vma=False,
    )
```

```python
import functools
import math

import jax
import jax.numpy as jnp
from jax import lax
from jax.experimental import pallas as pl
from jax.experimental.pallas import tpu as pltpu
from jax.sharding import PartitionSpec as P

SLAB_Z = 4
MAG_LOW, MAG_HIGH, SHIFT_MAX = 0.85, 0.95, 8.0
TILE = 512
F32 = jnp.float32
BF16 = jnp.bfloat16
MESH = pl.DeviceIdType.MESH


def dot(a, b):
    return jnp.dot(a, b, preferred_element_type=F32)


def silu_of_half(half):
    return half + half * jnp.tanh(half)


def iota(shape, dim):
    return lax.broadcasted_iota(jnp.int32, shape, dim)


def as_column(row):
    size = row.shape[1]
    spread = jnp.broadcast_to(row, (size, size))
    return jnp.sum(
        jnp.where(iota((size, size), 0) == iota((size, size), 1), spread, 0.0), axis=1, keepdims=True
    )


def by_row(ref, shape, period):
    index = iota(shape, 0) // 2
    value = jnp.full(shape, ref[0], F32)
    for a in range(1, period):
        value = jnp.where(index == a, ref[a], value)
    return value


def log2(size):
    assert size & (size - 1) == 0
    return size.bit_length() - 1


def split(value, size, count):
    quotient = jnp.zeros_like(value)
    for k in range(1, count):
        quotient = quotient + jnp.where(value >= k * size, 1, 0)
    return quotient, value - quotient * size


def store_shifted(ref, first_before, first_after, count, values):
    cols = values.shape[1]
    column = iota((count, 128), 1)
    zero = jnp.zeros((count, 128), values.dtype)
    before = pltpu.roll(values, 1, 1)
    after = pltpu.roll(values, cols - 1, 1)
    ref[pl.ds(first_before, count), pl.ds(128, cols - 128)] = before[:, 128:]
    ref[pl.ds(first_before, count), pl.ds(0, 128)] = jnp.where(column == 0, zero, before[:, :128])
    ref[pl.ds(first_after, count), pl.ds(0, cols - 128)] = after[:, : cols - 128]
    ref[pl.ds(first_after, count), pl.ds(cols - 128, 128)] = jnp.where(
        column == 127, zero, after[:, cols - 128 :]
    )


def kernel(
    n_ang, n_row, *refs,
):
    sources, (nd_out, vol_out), locals_ = refs[:13], refs[13:15], refs[15:28]
    dual, forward, sino, fw, fb, mw, mb, lw, mag, shift, frac, offsets, order = locals_
    (
    halo, x1, x1s, x2, x3, wrows, w1, w2, w3, ramp, frac_own, frac_all, sent, got,
    halo_send, halo_recv, frac_send, frac_recv, send_sem, recv_sem, local_sem,
    ) = refs[28:]
    loads = [
        pltpu.make_async_copy(source, goal, local_sem.at[n])
        for n, (source, goal) in enumerate(zip(sources, locals_))
    ]
    for load in loads:
        load.start()
    angs, rows, cols = dual.shape
    ch = mw.shape[2]
    total = n_ang * n_row
    my_ang, my_row = lax.axis_index("ang"), lax.axis_index("row")
    me = my_ang * n_row + my_row
    wide = angs + 6
    out1, out2 = angs + 4, angs + 2
    ar = angs * rows
    per = 64

    def place_of(step):
        target = lax.rem(me + step, total)
        return target, target // n_row, lax.rem(target, n_row)

    barrier = pltpu.get_barrier_semaphore()

    def greet(step, carry):
        _, ang, row = place_of(step)
        pl.semaphore_signal(barrier, inc=1, device_id=(ang, row), device_id_type=MESH)
        return carry

    lax.fori_loop(1, total, greet, 0)

    narrow = cols // 128

    def ramp_block(b):
        away = (b - (narrow - 1)) * 128 + iota((128, 128), 1) - iota((128, 128), 0)
        odd = (away & 1) == 1
        distance = jnp.where(odd, away, 1).astype(F32)
        value = jnp.where(odd, -1.0 / (math.pi * math.pi * distance * distance), 0.0)
        ramp[:, pl.ds(pl.multiple_of(b * 128, 128), 128)] = jnp.where(away == 0, 0.25, value).astype(BF16)

    pl.semaphore_wait(barrier, total - 1)

    left = lax.rem(my_ang + n_ang - 1, n_ang)
    right = lax.rem(my_ang + 1, n_ang)
    halo_copies = []
    for c, ref in enumerate(sources[:3]):
        for side, (peer, first) in enumerate(((right, angs - 3), (left, 0))):
            copy = pltpu.make_async_remote_copy(
                src_ref=ref.at[pl.ds(first, 3)],
                dst_ref=halo.at[side, c],
                send_sem=halo_send.at[side, c],
                recv_sem=halo_recv.at[side, c],
                device_id=(peer, my_row),
                device_id_type=MESH,
            )
            copy.start()
            halo_copies.append(copy)

    for load in loads:
        load.wait()
    lane = iota((8, 128), 1)
    mine = jnp.full((8, 128), frac[0], F32)
    for a in range(1, angs):
        mine = jnp.where((lane & (ar - 1)) // rows == a, frac[a], mine)
    frac_own[...] = mine
    frac_all[my_ang] = mine

    def frac_copy(source, target):
        return pltpu.make_async_remote_copy(
            src_ref=frac_own,
            dst_ref=frac_all.at[source],
            send_sem=frac_send.at[target],
            recv_sem=frac_recv.at[source],
            device_id=(target, my_row),
            device_id_type=MESH,
        )

    def frac_start(step, carry):
        frac_copy(my_ang, lax.rem(my_ang + step, n_ang)).start()
        return carry

    lax.fori_loop(1, n_ang, frac_start, 0)

    k1 = 3 * per
    tap1, rest1 = split(iota((ch, k1), 1), per, 3)
    chan1, rest1 = split(rest1, wide * rows, 4)
    ang1 = jnp.where(chan1 < 3, rest1 >> 1, -9)
    row1 = rest1 & 1
    for i in range(3):
        for j in range(3):
            wrows[pl.ds((i * 3 + j) * 3, 3), :] = fw[i, j].astype(F32)
    entry = iota((32, 4 * per), 0)
    tap_all, rest_all = split(iota((32, 4 * per), 1), per, 4)
    chan_all, _ = split(rest_all, wide * rows, 4)
    chosen = jnp.where(chan_all < 3, tap_all * 3 + chan_all, -99)
    chosen = jnp.where(tap_all < 3, chosen, -99)
    pick1 = jnp.concatenate(
        [jnp.where(entry == chosen + i * 9, 0.5, 0.0).astype(BF16) for i in range(3)], axis=1
    )
    entries = jnp.where(iota((32, ch), 0) < 27, wrows[...], 0.0).astype(BF16)
    tiles1 = lax.dot_general(entries, pick1, (((0,), (0,)), ((), ())), preferred_element_type=F32)
    joined1 = [tiles1[:, i * 4 * per : i * 4 * per + k1] for i in range(3)]
    bias1 = jnp.zeros((ch, k1), F32)
    left_over = as_column(fb[...]) * 0.5
    for n in range(3):
        part = left_over.astype(BF16).astype(F32)
        left_over = left_over - part
        bias1 = jnp.where(iota((ch, k1), 1) == per + 3 * wide * rows + n, part, bias1)
    for r in range(rows):
        for a in range(out1):
            block = bias1
            for i in range(3):
                block = jnp.where((ang1 == a + i) & (row1 == r), joined1[i], block)
            w1[pl.ds((r * out1 + a) * ch, ch), :] = block.astype(BF16)

    k2 = out1 * ch
    pick2 = jnp.where((iota((ch, k2), 1) & (ch - 1)) == iota((ch, k2), 0), 0.5, 0.0).astype(BF16)
    ang2, _ = split(iota((ch, k2), 1), ch, out1)
    all2 = dot(mw[...].reshape(9 * ch, ch), pick2)
    for j in range(3):
        tiles2 = [all2[(i * 3 + j) * ch : (i * 3 + j + 1) * ch] for i in range(3)]
        for a in range(out2):
            block = jnp.zeros((ch, k2), F32)
            for i in range(3):
                block = jnp.where(ang2 == a + i, tiles2[i], block)
            w2[pl.ds(a * ch, ch), pl.ds(j * k2, k2)] = block.astype(BF16)

    k3 = rows * out2 * ch
    pick3 = jnp.where((iota((ch, k3), 1) & (ch - 1)) == iota((ch, k3), 0), 1.0, 0.0).astype(BF16)
    row3, rest3 = split(iota((ar, k3), 1), out2 * ch, rows)
    ang3, _ = split(rest3, ch, out2)
    ang3 = ang3 - (iota((ar, k3), 0) >> 1)
    same3 = row3 == (iota((ar, k3), 0) & 1)
    spread3 = [
        jnp.broadcast_to(lw[i, 0, j : j + 1, :].astype(F32), (ar, ch)) for i in range(3) for j in range(3)
    ]
    all3 = dot(jnp.concatenate(spread3, axis=0).astype(BF16), pick3)
    blocks3 = []
    for j in range(3):
        block = jnp.zeros((ar, k3), F32)
        for i in range(3):
            at = (i * 3 + j) * ar
            block = jnp.where((ang3 == i) & same3, all3[at : at + ar], block)
        blocks3.append(block)
    blocks3.append(jnp.zeros((ar, k3), F32))
    w3[...] = jnp.concatenate(blocks3, axis=0).astype(BF16)

    bias2 = jnp.concatenate([as_column(mb[...]) * 0.5] * out2, axis=0)

    used = 3 * wide * rows
    x1[pl.ds(per - 8, 8), :] = jnp.where(iota((8, cols), 0) + per - 8 < used + 3, 1.0, 0.0)
    for c, ref in enumerate((dual, forward, sino)):
        for a in range(angs):
            x1[pl.ds((c * wide + 3 + a) * rows, rows), :] = ref[a].astype(F32)
    for copy in halo_copies:
        copy.wait()
    for c in range(3):
        for a in range(3):
            x1[pl.ds((c * wide + a) * rows, rows), :] = halo[0, c, a].astype(F32)
            x1[pl.ds((c * wide + 3 + angs + a) * rows, rows), :] = halo[1, c, a].astype(F32)
    middle = x1[...].astype(BF16)
    store_shifted(x1s, 0, 2 * per, per, middle)
    x1s[pl.ds(per, per), :] = middle
    tiles = cols // TILE

    def layer1(t, carry):
        start = pl.multiple_of(t * TILE, TILE)
        value = silu_of_half(dot(w1[...], x1s[:, pl.ds(start, TILE)])).astype(BF16)
        for r in range(rows):
            x2[pl.ds((r * 3 + 1) * k2, k2), pl.ds(start, TILE)] = value[r * k2 : (r + 1) * k2]
        return carry

    lax.fori_loop(0, tiles, layer1, 0)

    def shift2(n, carry):
        for r in range(rows):
            base = r * 3 * k2 + n * ch
            values = x2[pl.ds(pl.multiple_of(base + k2, ch), ch), :]
            store_shifted(
                x2, pl.multiple_of(base, ch), pl.multiple_of(base + 2 * k2, ch), ch, values
            )
        return carry

    lax.fori_loop(0, out1, shift2, 0)

    ramps = 2 * narrow // tiles

    def layer2(t, carry):
        start = pl.multiple_of(t * TILE, TILE)
        for r in range(rows):
            value = dot(w2[...], x2[pl.ds(r * 3 * k2, 3 * k2), pl.ds(start, TILE)]) + bias2
            x3[pl.ds(r * out2 * ch, out2 * ch), pl.ds(start, TILE)] = silu_of_half(value).astype(BF16)
        for n in range(ramps):
            ramp_block(t * ramps + n)
        return carry

    lax.fori_loop(0, tiles, layer2, 0)

    taps = dot(w3[...], x3[...])
    column = iota((ar, cols), 1)
    before = jnp.where(column == 0, 0.0, pltpu.roll(taps[0:ar], 1, 1))
    after = jnp.where(column == cols - 1, 0.0, pltpu.roll(taps[2 * ar : 3 * ar], cols - 1, 1))
    update = before + taps[ar : 2 * ar] + after
    own = x1[pl.ds(3 * rows, ar), :]
    new_dual = (own + update).astype(BF16).astype(F32)
    for a in range(angs):
        nd_out[a] = new_dual[a * rows : (a + 1) * rows].astype(BF16)

    pieces = jnp.concatenate(
        [new_dual[:, n * 128 : (n + 1) * 128] for n in range(narrow)], axis=0
    ).astype(BF16)
    lanes = [None] * narrow
    for pair in range(0, 2 * narrow - 1, 2):
        near = min(2, 2 * narrow - 1 - pair)
        product = dot(pieces, ramp[:, pl.ds(pair * 128, near * 128)])
        for b in range(pair, pair + near):
            for source in range(narrow):
                goal = source + b - (narrow - 1)
                if 0 <= goal < narrow:
                    at = (b - pair) * 128
                    part = product[source * ar : (source + 1) * ar, at : at + 128]
                    lanes[goal] = part if lanes[goal] is None else lanes[goal] + part

    centre = (cols - 1) / 2.0
    mags = by_row(mag, (ar, 128), angs)
    shifts = by_row(shift, (ar, 128), angs)
    halves = cols // n_ang // 128
    size = halves * ar

    def block_copy(source, target, ang, row):
        return pltpu.make_async_remote_copy(
            src_ref=sent.at[ang],
            dst_ref=got.at[source],
            send_sem=send_sem.at[target],
            recv_sem=recv_sem.at[source],
            device_id=(ang, row),
            device_id_type=MESH,
        )

    projected = []
    for n in range(cols // 128):
        edges = [
            (x - centre) * m + centre + s
            for x in (n * 128, n * 128 + 127)
            for m in (MAG_LOW, MAG_HIGH)
            for s in (-SHIFT_MAX, SHIFT_MAX)
        ]
        lowest = max(int((min(edges) - 0.1) // 128), 0)
        highest = min(int((max(edges) + 1.1) // 128), cols // 128 - 1)
        places = ((iota((ar, 128), 1) + n * 128).astype(F32) - centre) * mags + centre + shifts
        floors = jnp.floor(places)
        weight = places - floors
        low = floors.astype(jnp.int32)
        ends = []
        for index in (low, low + 1):
            value = jnp.zeros((ar, 128), F32)
            for k in range(lowest, highest + 1):
                taken = jnp.take_along_axis(lanes[k], index & 127, axis=1)
                value = jnp.where(index >> 7 == k, taken, value)
            ends.append(value)
        projected.append((1.0 - weight) * ends[0] + weight * ends[1])
        if len(projected) == halves:
            p = n // halves
            sent[p] = jnp.concatenate(projected, axis=0).astype(BF16)
            projected = []
            for step in range(1, n_row):
                row = lax.rem(my_row + step, n_row)
                block_copy(me, p * n_row + row, p, row).start()

            @pl.when(my_ang != p)
            def _():
                block_copy(me, p * n_row + my_row, p, my_row).start()


    got[me] = sent[my_ang]

    def frac_wait(step, carry):
        peer = lax.rem(my_ang + step, n_ang)
        frac_copy(peer, peer).wait()
        return carry

    lax.fori_loop(1, n_ang, frac_wait, 0)

    slots = order.shape[0] // n_row
    depth = total * size
    zs = slots * SLAB_Z
    place = iota((zs, depth), 1)
    level = iota((zs, depth), 0)
    source_ang = (place >> log2(n_row * size))
    piece_row = ((place >> log2(size)) & (n_row - 1)) * rows + (place & (rows - 1))
    half_of = ((place & (size - 1)) >> log2(ar))
    starts = jnp.zeros((zs, depth), jnp.int32)
    fraction = jnp.zeros((zs, depth), F32)
    for p in range(n_ang):
        here = source_ang == p
        spread = jnp.concatenate([frac_all[p][0:1]] * (depth // 128), axis=1)
        fraction = jnp.where(here, jnp.broadcast_to(spread, (zs, depth)), fraction)
        for k in range(slots):
            first = offsets[p, order[my_row * slots + k]]
            starts = jnp.where(here & ((level >> log2(SLAB_Z)) == k), first, starts)
    reach = piece_row - starts - (level & (SLAB_Z - 1))
    weights = jnp.where(reach == 0, 1.0 - fraction, jnp.where(reach == 1, fraction, 0.0))
    parts = []
    for h in range(halves):
        left_over = jnp.where(half_of == h, weights, 0.0)
        for _ in range(3):
            part = left_over.astype(BF16)
            left_over = left_over - part.astype(F32)
            parts.append(part)
    stacked = jnp.concatenate(parts, axis=0)

    def block_wait(step, carry):
        target, ang, row = place_of(step)
        block_copy(target, target, ang, row).wait()
        return carry

    lax.fori_loop(1, total, block_wait, 0)

    sums = dot(stacked, got[...].reshape(depth, 128))
    for h in range(halves):
        three = [sums[(h * 3 + s) * zs : (h * 3 + s + 1) * zs] for s in range(3)]
        vol_out[:, pl.ds(h * 128, 128)] = (three[2] + three[1] + three[0]) / math.sqrt(n_ang * angs)


def per_device(
    n_ang, n_row, dual_field, forward, sinogram, first_weight, first_bias, middle_weight,
    middle_bias, last_weight, magnify, detector_shift, row_fraction, offsets, slab_order,
):
    angs, rows, cols = dual_field.shape
    ch = first_weight.shape[2]
    operands = (
        dual_field, forward, sinogram, first_weight.transpose(0, 1, 3, 2), first_bias[None, :],
        middle_weight, middle_bias[None, :], last_weight.transpose(0, 2, 1, 3), magnify,
        detector_shift, row_fraction, offsets, slab_order,
    )
    total = n_ang * n_row
    ar = angs * rows
    out1, out2 = angs + 4, angs + 2
    narrow = cols // 128
    width = cols // n_ang
    size = width // 128 * ar
    slots = slab_order.shape[0] // n_row
    vmem = pl.BlockSpec(memory_space=pltpu.VMEM)
    dma = pltpu.SemaphoreType.DMA
    return pl.pallas_call(
        functools.partial(kernel, n_ang, n_row),
        out_shape=(
            jax.ShapeDtypeStruct(dual_field.shape, BF16),
            jax.ShapeDtypeStruct((slots * SLAB_Z, width), F32),
        ),
        in_specs=[pl.BlockSpec(memory_space=pltpu.HBM)] * 13,
        out_specs=(vmem, vmem),
        scratch_shapes=[pltpu.VMEM(x.shape, x.dtype) for x in operands[:8]]
        + [pltpu.SMEM(x.shape, x.dtype) for x in operands[8:]]
        + [
            pltpu.VMEM((2, 3, 3, rows, cols), BF16),
            pltpu.VMEM((64, cols), F32),
            pltpu.VMEM((3 * 64, cols), BF16),
            pltpu.VMEM((rows * 3 * out1 * ch, cols), BF16),
            pltpu.VMEM((rows * out2 * ch, cols), BF16),
            pltpu.VMEM((32, ch), F32),
            pltpu.VMEM((rows * out1 * ch, 3 * 64), BF16),
            pltpu.VMEM((out2 * ch, 3 * out1 * ch), BF16),
            pltpu.VMEM((4 * ar, rows * out2 * ch), BF16),
            pltpu.VMEM((128, 2 * narrow * 128), BF16),
            pltpu.VMEM((8, 128), F32),
            pltpu.VMEM((n_ang, 8, 128), F32),
            pltpu.VMEM((n_ang, size, 128), BF16),
            pltpu.VMEM((total, size, 128), BF16),
            dma((2, 3)),
            dma((2, 3)),
            dma((n_ang,)),
            dma((n_ang,)),
            dma((total,)),
            dma((total,)),
            dma((13,)),
        ],
        compiler_params=pltpu.CompilerParams(
            collective_id=0, has_side_effects=True, vmem_limit_bytes=65280 * 1024
        ),
        cost_estimate=pl.CostEstimate(flops=10**9, bytes_accessed=10**6, transcendentals=0),
    )(*operands)


def solution(mesh):
    sizes = dict(mesh.shape)
    split = P("ang", "row", None)
    return jax.shard_map(
        functools.partial(per_device, sizes["ang"], sizes["row"]),
        mesh=mesh,
        in_specs=(
            split, split, split, P(), P(), P(), P(), P(), P("ang"), P("ang"), P("ang"), P(), P(),
        ),
        out_specs=(split, P("row", "ang")),
        check_vma=False,
    )
```

```python
import functools
import math

import jax
import jax.numpy as jnp
from jax import lax
from jax.experimental import pallas as pl
from jax.experimental.pallas import tpu as pltpu
from jax.sharding import PartitionSpec as P

SLAB_Z = 4
MAG_LOW, MAG_HIGH, SHIFT_MAX = 0.85, 0.95, 8.0
TILE = 512
F32 = jnp.float32
BF16 = jnp.bfloat16
MESH = pl.DeviceIdType.MESH


def dot(a, b):
    return jnp.dot(a, b, preferred_element_type=F32)


def silu_of_half(half):
    return half + half * jnp.tanh(half)


def iota(shape, dim):
    return lax.broadcasted_iota(jnp.int32, shape, dim)


def as_column(row):
    size = row.shape[1]
    spread = jnp.broadcast_to(row, (size, size))
    return jnp.sum(
        jnp.where(iota((size, size), 0) == iota((size, size), 1), spread, 0.0), axis=1, keepdims=True
    )


def by_row(ref, shape, period):
    index = iota(shape, 0) // 2
    value = jnp.full(shape, ref[0], F32)
    for a in range(1, period):
        value = jnp.where(index == a, ref[a], value)
    return value


def log2(size):
    assert size & (size - 1) == 0
    return size.bit_length() - 1


def split(value, size, count):
    quotient = jnp.zeros_like(value)
    for k in range(1, count):
        quotient = quotient + jnp.where(value >= k * size, 1, 0)
    return quotient, value - quotient * size


def store_shifted(ref, first_before, first_after, count, values):
    cols = values.shape[1]
    column = iota((count, 128), 1)
    zero = jnp.zeros((count, 128), values.dtype)
    before = pltpu.roll(values, 1, 1)
    after = pltpu.roll(values, cols - 1, 1)
    ref[pl.ds(first_before, count), pl.ds(128, cols - 128)] = before[:, 128:]
    ref[pl.ds(first_before, count), pl.ds(0, 128)] = jnp.where(column == 0, zero, before[:, :128])
    ref[pl.ds(first_after, count), pl.ds(0, cols - 128)] = after[:, : cols - 128]
    ref[pl.ds(first_after, count), pl.ds(cols - 128, 128)] = jnp.where(
        column == 127, zero, after[:, cols - 128 :]
    )


def kernel(
    n_ang, n_row, *refs,
):
    sources, (nd_out, vol_out), locals_ = refs[:13], refs[13:15], refs[15:28]
    dual, forward, sino, fw, fb, mw, mb, lw, mag, shift, frac, offsets, order = locals_
    (
    halo, x1, x1s, x2, x3, wrows, w1, w2, w3, ramp, frac_own, frac_all, sent, got,
    halo_send, halo_recv, frac_send, frac_recv, send_sem, recv_sem, local_sem,
    ) = refs[28:]
    loads = [
        pltpu.make_async_copy(source, goal, local_sem.at[n])
        for n, (source, goal) in enumerate(zip(sources, locals_))
    ]
    angs, rows, cols = dual.shape
    ch = mw.shape[2]
    total = n_ang * n_row
    my_ang, my_row = lax.axis_index("ang"), lax.axis_index("row")
    me = my_ang * n_row + my_row
    wide = angs + 6
    out1, out2 = angs + 4, angs + 2
    ar = angs * rows
    per = 64

    def place_of(step):
        target = lax.rem(me + step, total)
        return target, target // n_row, lax.rem(target, n_row)

    barrier = pltpu.get_barrier_semaphore()

    def greet(step, carry):
        _, ang, row = place_of(step)
        pl.semaphore_signal(barrier, inc=1, device_id=(ang, row), device_id_type=MESH)
        return carry

    lax.fori_loop(1, total, greet, 0)
    for load in loads:
        load.start()

    narrow = cols // 128

    def ramp_block(b):
        away = (b - (narrow - 1)) * 128 + iota((128, 128), 1) - iota((128, 128), 0)
        odd = (away & 1) == 1
        distance = jnp.where(odd, away, 1).astype(F32)
        value = jnp.where(odd, -1.0 / (math.pi * math.pi * distance * distance), 0.0)
        ramp[:, pl.ds(pl.multiple_of(b * 128, 128), 128)] = jnp.where(away == 0, 0.25, value).astype(BF16)

    pl.semaphore_wait(barrier, total - 1)

    left = lax.rem(my_ang + n_ang - 1, n_ang)
    right = lax.rem(my_ang + 1, n_ang)
    halo_copies = []
    for c, ref in enumerate(sources[:3]):
        for side, (peer, first) in enumerate(((right, angs - 3), (left, 0))):
            copy = pltpu.make_async_remote_copy(
                src_ref=ref.at[pl.ds(first, 3)],
                dst_ref=halo.at[side, c],
                send_sem=halo_send.at[side, c],
                recv_sem=halo_recv.at[side, c],
                device_id=(peer, my_row),
                device_id_type=MESH,
            )
            copy.start()
            halo_copies.append(copy)

    for load in loads:
        load.wait()
    lane = iota((8, 128), 1)
    mine = jnp.full((8, 128), frac[0], F32)
    for a in range(1, angs):
        mine = jnp.where((lane & (ar - 1)) // rows == a, frac[a], mine)
    frac_own[...] = mine
    frac_all[my_ang] = mine

    def frac_copy(source, target):
        return pltpu.make_async_remote_copy(
            src_ref=frac_own,
            dst_ref=frac_all.at[source],
            send_sem=frac_send.at[target],
            recv_sem=frac_recv.at[source],
            device_id=(target, my_row),
            device_id_type=MESH,
        )

    def frac_start(step, carry):
        frac_copy(my_ang, lax.rem(my_ang + step, n_ang)).start()
        return carry

    lax.fori_loop(1, n_ang, frac_start, 0)

    k1 = 3 * per
    tap1, rest1 = split(iota((ch, k1), 1), per, 3)
    chan1, rest1 = split(rest1, wide * rows, 4)
    ang1 = jnp.where(chan1 < 3, rest1 >> 1, -9)
    row1 = rest1 & 1
    for i in range(3):
        for j in range(3):
            wrows[pl.ds((i * 3 + j) * 3, 3), :] = fw[i, j].astype(F32)
    entry = iota((32, 4 * per), 0)
    tap_all, rest_all = split(iota((32, 4 * per), 1), per, 4)
    chan_all, _ = split(rest_all, wide * rows, 4)
    chosen = jnp.where(chan_all < 3, tap_all * 3 + chan_all, -99)
    chosen = jnp.where(tap_all < 3, chosen, -99)
    pick1 = jnp.concatenate(
        [jnp.where(entry == chosen + i * 9, 0.5, 0.0).astype(BF16) for i in range(3)], axis=1
    )
    entries = jnp.where(iota((32, ch), 0) < 27, wrows[...], 0.0).astype(BF16)
    tiles1 = lax.dot_general(entries, pick1, (((0,), (0,)), ((), ())), preferred_element_type=F32)
    joined1 = [tiles1[:, i * 4 * per : i * 4 * per + k1] for i in range(3)]
    bias1 = jnp.zeros((ch, k1), F32)
    left_over = as_column(fb[...]) * 0.5
    for n in range(3):
        part = left_over.astype(BF16).astype(F32)
        left_over = left_over - part
        bias1 = jnp.where(iota((ch, k1), 1) == per + 3 * wide * rows + n, part, bias1)
    for r in range(rows):
        for a in range(out1):
            block = bias1
            for i in range(3):
                block = jnp.where((ang1 == a + i) & (row1 == r), joined1[i], block)
            w1[pl.ds((r * out1 + a) * ch, ch), :] = block.astype(BF16)

    k2 = out1 * ch
    pick2 = jnp.where((iota((ch, k2), 1) & (ch - 1)) == iota((ch, k2), 0), 0.5, 0.0).astype(BF16)
    ang2, _ = split(iota((ch, k2), 1), ch, out1)
    all2 = dot(mw[...].reshape(9 * ch, ch), pick2)
    for j in range(3):
        tiles2 = [all2[(i * 3 + j) * ch : (i * 3 + j + 1) * ch] for i in range(3)]
        for a in range(out2):
            block = jnp.zeros((ch, k2), F32)
            for i in range(3):
                block = jnp.where(ang2 == a + i, tiles2[i], block)
            w2[pl.ds(a * ch, ch), pl.ds(j * k2, k2)] = block.astype(BF16)

    k3 = rows * out2 * ch
    pick3 = jnp.where((iota((ch, k3), 1) & (ch - 1)) == iota((ch, k3), 0), 1.0, 0.0).astype(BF16)
    row3, rest3 = split(iota((ar, k3), 1), out2 * ch, rows)
    ang3, _ = split(rest3, ch, out2)
    ang3 = ang3 - (iota((ar, k3), 0) >> 1)
    same3 = row3 == (iota((ar, k3), 0) & 1)
    spread3 = [
        jnp.broadcast_to(lw[i, 0, j : j + 1, :].astype(F32), (ar, ch)) for i in range(3) for j in range(3)
    ]
    all3 = dot(jnp.concatenate(spread3, axis=0).astype(BF16), pick3)
    blocks3 = []
    for j in range(3):
        block = jnp.zeros((ar, k3), F32)
        for i in range(3):
            at = (i * 3 + j) * ar
            block = jnp.where((ang3 == i) & same3, all3[at : at + ar], block)
        blocks3.append(block)
    blocks3.append(jnp.zeros((ar, k3), F32))
    w3[...] = jnp.concatenate(blocks3, axis=0).astype(BF16)

    bias2 = jnp.concatenate([as_column(mb[...]) * 0.5] * out2, axis=0)

    used = 3 * wide * rows
    x1[pl.ds(per - 8, 8), :] = jnp.where(iota((8, cols), 0) + per - 8 < used + 3, 1.0, 0.0)
    for c, ref in enumerate((dual, forward, sino)):
        for a in range(angs):
            x1[pl.ds((c * wide + 3 + a) * rows, rows), :] = ref[a].astype(F32)
    for copy in halo_copies:
        copy.wait()
    for c in range(3):
        for a in range(3):
            x1[pl.ds((c * wide + a) * rows, rows), :] = halo[0, c, a].astype(F32)
            x1[pl.ds((c * wide + 3 + angs + a) * rows, rows), :] = halo[1, c, a].astype(F32)
    middle = x1[...].astype(BF16)
    store_shifted(x1s, 0, 2 * per, per, middle)
    x1s[pl.ds(per, per), :] = middle
    tiles = cols // TILE

    def layer1(t, carry):
        start = pl.multiple_of(t * TILE, TILE)
        value = silu_of_half(dot(w1[...], x1s[:, pl.ds(start, TILE)])).astype(BF16)
        before = pltpu.roll(value, 1, 1)
        after = pltpu.roll(value, TILE - 1, 1)
        for r in range(rows):
            for j, whole in enumerate((before, value, after)):
                x2[pl.ds((r * 3 + j) * k2, k2), pl.ds(start, TILE)] = whole[r * k2 : (r + 1) * k2]
        return carry

    lax.fori_loop(0, tiles, layer1, 0)

    edge = iota((k2, 128), 1)
    zero = jnp.zeros((k2, 128), BF16)
    for r in range(rows):
        low, mid, high = [pl.ds((r * 3 + j) * k2, k2) for j in range(3)]
        for t in range(tiles):
            first, last = pl.ds(t * TILE, 128), pl.ds((t + 1) * TILE - 128, 128)
            beyond = zero
            if t > 0:
                beyond = pltpu.roll(x2[mid, pl.ds(t * TILE - 128, 128)], 1, 1)
            x2[low, first] = jnp.where(edge == 0, beyond, x2[low, first])
            beyond = zero
            if t < tiles - 1:
                beyond = pltpu.roll(x2[mid, pl.ds((t + 1) * TILE, 128)], 127, 1)
            x2[high, last] = jnp.where(edge == 127, beyond, x2[high, last])

    ramps = 2 * narrow // tiles

    def layer2(t, carry):
        start = pl.multiple_of(t * TILE, TILE)
        for r in range(rows):
            value = dot(w2[...], x2[pl.ds(r * 3 * k2, 3 * k2), pl.ds(start, TILE)]) + bias2
            x3[pl.ds(r * out2 * ch, out2 * ch), pl.ds(start, TILE)] = silu_of_half(value).astype(BF16)
        for n in range(ramps):
            ramp_block(t * ramps + n)
        return carry

    lax.fori_loop(0, tiles, layer2, 0)

    taps = dot(w3[...], x3[...])
    column = iota((ar, cols), 1)
    before = jnp.where(column == 0, 0.0, pltpu.roll(taps[0:ar], 1, 1))
    after = jnp.where(column == cols - 1, 0.0, pltpu.roll(taps[2 * ar : 3 * ar], cols - 1, 1))
    update = before + taps[ar : 2 * ar] + after
    own = x1[pl.ds(3 * rows, ar), :]
    new_dual = (own + update).astype(BF16).astype(F32)
    for a in range(angs):
        nd_out[a] = new_dual[a * rows : (a + 1) * rows].astype(BF16)

    pieces = jnp.concatenate(
        [new_dual[:, n * 128 : (n + 1) * 128] for n in range(narrow)], axis=0
    ).astype(BF16)
    lanes = [None] * narrow
    for pair in range(0, 2 * narrow - 1, 2):
        near = min(2, 2 * narrow - 1 - pair)
        product = dot(pieces, ramp[:, pl.ds(pair * 128, near * 128)])
        for b in range(pair, pair + near):
            for source in range(narrow):
                goal = source + b - (narrow - 1)
                if 0 <= goal < narrow:
                    at = (b - pair) * 128
                    part = product[source * ar : (source + 1) * ar, at : at + 128]
                    lanes[goal] = part if lanes[goal] is None else lanes[goal] + part

    centre = (cols - 1) / 2.0
    mags = by_row(mag, (ar, 128), angs)
    shifts = by_row(shift, (ar, 128), angs)
    halves = cols // n_ang // 128
    size = halves * ar

    def block_copy(source, target, ang, row):
        return pltpu.make_async_remote_copy(
            src_ref=sent.at[ang],
            dst_ref=got.at[source],
            send_sem=send_sem.at[target],
            recv_sem=recv_sem.at[source],
            device_id=(ang, row),
            device_id_type=MESH,
        )

    projected = []
    for n in range(cols // 128):
        edges = [
            (x - centre) * m + centre + s
            for x in (n * 128, n * 128 + 127)
            for m in (MAG_LOW, MAG_HIGH)
            for s in (-SHIFT_MAX, SHIFT_MAX)
        ]
        lowest = max(int((min(edges) - 0.1) // 128), 0)
        highest = min(int((max(edges) + 1.1) // 128), cols // 128 - 1)
        places = ((iota((ar, 128), 1) + n * 128).astype(F32) - centre) * mags + centre + shifts
        floors = jnp.floor(places)
        weight = places - floors
        low = floors.astype(jnp.int32)
        ends = []
        for index in (low, low + 1):
            value = jnp.zeros((ar, 128), F32)
            for k in range(lowest, highest + 1):
                taken = jnp.take_along_axis(lanes[k], index & 127, axis=1)
                value = jnp.where(index >> 7 == k, taken, value)
            ends.append(value)
        projected.append((1.0 - weight) * ends[0] + weight * ends[1])
        if len(projected) == halves:
            p = n // halves
            sent[p] = jnp.concatenate(projected, axis=0).astype(BF16)
            projected = []
            for step in range(1, n_row):
                row = lax.rem(my_row + step, n_row)
                block_copy(me, p * n_row + row, p, row).start()

            @pl.when(my_ang != p)
            def _():
                block_copy(me, p * n_row + my_row, p, my_row).start()


    got[me] = sent[my_ang]

    def frac_wait(step, carry):
        peer = lax.rem(my_ang + step, n_ang)
        frac_copy(peer, peer).wait()
        return carry

    lax.fori_loop(1, n_ang, frac_wait, 0)

    slots = order.shape[0] // n_row
    depth = total * size
    zs = slots * SLAB_Z
    place = iota((zs, depth), 1)
    level = iota((zs, depth), 0)
    source_ang = (place >> log2(n_row * size))
    piece_row = ((place >> log2(size)) & (n_row - 1)) * rows + (place & (rows - 1))
    half_of = ((place & (size - 1)) >> log2(ar))
    starts = jnp.zeros((zs, depth), jnp.int32)
    fraction = jnp.zeros((zs, depth), F32)
    for p in range(n_ang):
        here = source_ang == p
        spread = jnp.concatenate([frac_all[p][0:1]] * (depth // 128), axis=1)
        fraction = jnp.where(here, jnp.broadcast_to(spread, (zs, depth)), fraction)
        for k in range(slots):
            first = offsets[p, order[my_row * slots + k]]
            starts = jnp.where(here & ((level >> log2(SLAB_Z)) == k), first, starts)
    reach = piece_row - starts - (level & (SLAB_Z - 1))
    weights = jnp.where(reach == 0, 1.0 - fraction, jnp.where(reach == 1, fraction, 0.0))
    parts = []
    for h in range(halves):
        left_over = jnp.where(half_of == h, weights, 0.0)
        for _ in range(3):
            part = left_over.astype(BF16)
            left_over = left_over - part.astype(F32)
            parts.append(part)
    stacked = jnp.concatenate(parts, axis=0)

    def block_wait(step, carry):
        target, ang, row = place_of(step)
        block_copy(target, target, ang, row).wait()
        return carry

    lax.fori_loop(1, total, block_wait, 0)

    sums = dot(stacked, got[...].reshape(depth, 128))
    for h in range(halves):
        three = [sums[(h * 3 + s) * zs : (h * 3 + s + 1) * zs] for s in range(3)]
        vol_out[:, pl.ds(h * 128, 128)] = (three[2] + three[1] + three[0]) / math.sqrt(n_ang * angs)


def per_device(
    n_ang, n_row, dual_field, forward, sinogram, first_weight, first_bias, middle_weight,
    middle_bias, last_weight, magnify, detector_shift, row_fraction, offsets, slab_order,
):
    angs, rows, cols = dual_field.shape
    ch = first_weight.shape[2]
    operands = (
        dual_field, forward, sinogram, first_weight.transpose(0, 1, 3, 2), first_bias[None, :],
        middle_weight, middle_bias[None, :], last_weight.transpose(0, 2, 1, 3), magnify,
        detector_shift, row_fraction, offsets, slab_order,
    )
    total = n_ang * n_row
    ar = angs * rows
    out1, out2 = angs + 4, angs + 2
    narrow = cols // 128
    width = cols // n_ang
    size = width // 128 * ar
    slots = slab_order.shape[0] // n_row
    vmem = pl.BlockSpec(memory_space=pltpu.VMEM)
    dma = pltpu.SemaphoreType.DMA
    return pl.pallas_call(
        functools.partial(kernel, n_ang, n_row),
        out_shape=(
            pltpu.VMEM(dual_field.shape, BF16),
            pltpu.VMEM((slots * SLAB_Z, width), F32),
        ),
        in_specs=[pl.BlockSpec(memory_space=pltpu.HBM)] * 13,
        out_specs=(vmem, vmem),
        scratch_shapes=[pltpu.VMEM(x.shape, x.dtype) for x in operands[:8]]
        + [pltpu.SMEM(x.shape, x.dtype) for x in operands[8:]]
        + [
            pltpu.VMEM((2, 3, 3, rows, cols), BF16),
            pltpu.VMEM((64, cols), F32),
            pltpu.VMEM((3 * 64, cols), BF16),
            pltpu.VMEM((rows * 3 * out1 * ch, cols), BF16),
            pltpu.VMEM((rows * out2 * ch, cols), BF16),
            pltpu.VMEM((32, ch), F32),
            pltpu.VMEM((rows * out1 * ch, 3 * 64), BF16),
            pltpu.VMEM((out2 * ch, 3 * out1 * ch), BF16),
            pltpu.VMEM((4 * ar, rows * out2 * ch), BF16),
            pltpu.VMEM((128, 2 * narrow * 128), BF16),
            pltpu.VMEM((8, 128), F32),
            pltpu.VMEM((n_ang, 8, 128), F32),
            pltpu.VMEM((n_ang, size, 128), BF16),
            pltpu.VMEM((total, size, 128), BF16),
            dma((2, 3)),
            dma((2, 3)),
            dma((n_ang,)),
            dma((n_ang,)),
            dma((total,)),
            dma((total,)),
            dma((13,)),
        ],
        compiler_params=pltpu.CompilerParams(
            collective_id=0, has_side_effects=True, vmem_limit_bytes=65280 * 1024
        ),
        cost_estimate=pl.CostEstimate(flops=10**9, bytes_accessed=10**6, transcendentals=0),
    )(*operands)


def solution(mesh):
    sizes = dict(mesh.shape)
    split = P("ang", "row", None)
    return jax.shard_map(
        functools.partial(per_device, sizes["ang"], sizes["row"]),
        mesh=mesh,
        in_specs=(
            split, split, split, P(), P(), P(), P(), P(), P("ang"), P("ang"), P("ang"), P(), P(),
        ),
        out_specs=(split, P("row", "ang")),
        check_vma=False,
    )
```

```python
import functools
import math

import jax
import jax.numpy as jnp
from jax import lax
from jax.experimental import pallas as pl
from jax.experimental.pallas import tpu as pltpu
from jax.sharding import PartitionSpec as P

SLAB_Z = 4
MAG_LOW, MAG_HIGH, SHIFT_MAX = 0.85, 0.95, 8.0
TILE = 512
F32 = jnp.float32
BF16 = jnp.bfloat16
MESH = pl.DeviceIdType.MESH


def dot(a, b):
    return jnp.dot(a, b, preferred_element_type=F32)


def silu_of_half(half):
    return half + half * jnp.tanh(half)


def iota(shape, dim):
    return lax.broadcasted_iota(jnp.int32, shape, dim)


def as_column(row):
    size = row.shape[1]
    spread = jnp.broadcast_to(row, (size, size))
    return jnp.sum(
        jnp.where(iota((size, size), 0) == iota((size, size), 1), spread, 0.0), axis=1, keepdims=True
    )


def by_row(ref, shape, period):
    index = iota(shape, 0) // 2
    value = jnp.full(shape, ref[0], F32)
    for a in range(1, period):
        value = jnp.where(index == a, ref[a], value)
    return value


def log2(size):
    assert size & (size - 1) == 0
    return size.bit_length() - 1


def split(value, size, count):
    quotient = jnp.zeros_like(value)
    for k in range(1, count):
        quotient = quotient + jnp.where(value >= k * size, 1, 0)
    return quotient, value - quotient * size


def store_shifted(ref, first_before, first_after, count, values):
    cols = values.shape[1]
    column = iota((count, 128), 1)
    zero = jnp.zeros((count, 128), values.dtype)
    before = pltpu.roll(values, 1, 1)
    after = pltpu.roll(values, cols - 1, 1)
    ref[pl.ds(first_before, count), pl.ds(128, cols - 128)] = before[:, 128:]
    ref[pl.ds(first_before, count), pl.ds(0, 128)] = jnp.where(column == 0, zero, before[:, :128])
    ref[pl.ds(first_after, count), pl.ds(0, cols - 128)] = after[:, : cols - 128]
    ref[pl.ds(first_after, count), pl.ds(cols - 128, 128)] = jnp.where(
        column == 127, zero, after[:, cols - 128 :]
    )


def kernel(
    n_ang, n_row, *refs,
):
    sources, (nd_out, vol_out), locals_ = refs[:13], refs[13:15], refs[15:28]
    dual, forward, sino, fw, fb, mw, mb, lw, mag, shift, frac, offsets, order = locals_
    (
    halo, x1, x1s, x2, x3, wrows, w1, w2, w3, ramp, frac_own, frac_all, sent, got,
    halo_send, halo_recv, frac_send, frac_recv, send_sem, recv_sem, local_sem,
    ) = refs[28:]
    loads = [
        pltpu.make_async_copy(source, goal, local_sem.at[n])
        for n, (source, goal) in enumerate(zip(sources, locals_))
    ]
    angs, rows, cols = dual.shape
    ch = mw.shape[2]
    total = n_ang * n_row
    my_ang, my_row = lax.axis_index("ang"), lax.axis_index("row")
    me = my_ang * n_row + my_row
    wide = angs + 6
    out1, out2 = angs + 4, angs + 2
    ar = angs * rows
    per = 64

    def place_of(step):
        target = lax.rem(me + step, total)
        return target, target // n_row, lax.rem(target, n_row)

    barrier = pltpu.get_barrier_semaphore()

    def greet(step, carry):
        _, ang, row = place_of(step)
        pl.semaphore_signal(barrier, inc=1, device_id=(ang, row), device_id_type=MESH)
        return carry

    lax.fori_loop(1, total, greet, 0)
    for load in loads:
        load.start()

    narrow = cols // 128

    def ramp_block(b):
        away = (b - (narrow - 1)) * 128 + iota((128, 128), 1) - iota((128, 128), 0)
        odd = (away & 1) == 1
        distance = jnp.where(odd, away, 1).astype(F32)
        value = jnp.where(odd, -1.0 / (math.pi * math.pi * distance * distance), 0.0)
        ramp[:, pl.ds(pl.multiple_of(b * 128, 128), 128)] = jnp.where(away == 0, 0.25, value).astype(BF16)

    for load in loads:
        load.wait()
    k1 = 3 * per
    tap1, rest1 = split(iota((ch, k1), 1), per, 3)
    chan1, rest1 = split(rest1, wide * rows, 4)
    ang1 = jnp.where(chan1 < 3, rest1 >> 1, -9)
    row1 = rest1 & 1
    for i in range(3):
        for j in range(3):
            wrows[pl.ds((i * 3 + j) * 3, 3), :] = fw[i, j].astype(F32)
    entry = iota((32, 4 * per), 0)
    tap_all, rest_all = split(iota((32, 4 * per), 1), per, 4)
    chan_all, _ = split(rest_all, wide * rows, 4)
    chosen = jnp.where(chan_all < 3, tap_all * 3 + chan_all, -99)
    chosen = jnp.where(tap_all < 3, chosen, -99)
    pick1 = jnp.concatenate(
        [jnp.where(entry == chosen + i * 9, 0.5, 0.0).astype(BF16) for i in range(3)], axis=1
    )
    entries = jnp.where(iota((32, ch), 0) < 27, wrows[...], 0.0).astype(BF16)
    tiles1 = lax.dot_general(entries, pick1, (((0,), (0,)), ((), ())), preferred_element_type=F32)
    joined1 = [tiles1[:, i * 4 * per : i * 4 * per + k1] for i in range(3)]
    bias1 = jnp.zeros((ch, k1), F32)
    left_over = as_column(fb[...]) * 0.5
    for n in range(3):
        part = left_over.astype(BF16).astype(F32)
        left_over = left_over - part
        bias1 = jnp.where(iota((ch, k1), 1) == per + 3 * wide * rows + n, part, bias1)
    for r in range(rows):
        for a in range(out1):
            block = bias1
            for i in range(3):
                block = jnp.where((ang1 == a + i) & (row1 == r), joined1[i], block)
            w1[pl.ds((r * out1 + a) * ch, ch), :] = block.astype(BF16)

    k3 = rows * out2 * ch
    pick3 = jnp.where((iota((ch, k3), 1) & (ch - 1)) == iota((ch, k3), 0), 1.0, 0.0).astype(BF16)
    row3, rest3 = split(iota((ar, k3), 1), out2 * ch, rows)
    ang3, _ = split(rest3, ch, out2)
    ang3 = ang3 - (iota((ar, k3), 0) >> 1)
    same3 = row3 == (iota((ar, k3), 0) & 1)
    spread3 = [
        jnp.broadcast_to(lw[i, 0, j : j + 1, :].astype(F32), (ar, ch)) for i in range(3) for j in range(3)
    ]
    all3 = dot(jnp.concatenate(spread3, axis=0).astype(BF16), pick3)
    blocks3 = []
    for j in range(3):
        block = jnp.zeros((ar, k3), F32)
        for i in range(3):
            at = (i * 3 + j) * ar
            block = jnp.where((ang3 == i) & same3, all3[at : at + ar], block)
        blocks3.append(block)
    blocks3.append(jnp.zeros((ar, k3), F32))
    w3[...] = jnp.concatenate(blocks3, axis=0).astype(BF16)

    pl.semaphore_wait(barrier, total - 1)

    left = lax.rem(my_ang + n_ang - 1, n_ang)
    right = lax.rem(my_ang + 1, n_ang)
    halo_copies = []
    for c, ref in enumerate(sources[:3]):
        for side, (peer, first) in enumerate(((right, angs - 3), (left, 0))):
            copy = pltpu.make_async_remote_copy(
                src_ref=ref.at[pl.ds(first, 3)],
                dst_ref=halo.at[side, c],
                send_sem=halo_send.at[side, c],
                recv_sem=halo_recv.at[side, c],
                device_id=(peer, my_row),
                device_id_type=MESH,
            )
            copy.start()
            halo_copies.append(copy)

    lane = iota((8, 128), 1)
    mine = jnp.full((8, 128), frac[0], F32)
    for a in range(1, angs):
        mine = jnp.where((lane & (ar - 1)) // rows == a, frac[a], mine)
    frac_own[...] = mine
    frac_all[my_ang] = mine

    def frac_copy(source, target):
        return pltpu.make_async_remote_copy(
            src_ref=frac_own,
            dst_ref=frac_all.at[source],
            send_sem=frac_send.at[target],
            recv_sem=frac_recv.at[source],
            device_id=(target, my_row),
            device_id_type=MESH,
        )

    def frac_start(step, carry):
        frac_copy(my_ang, lax.rem(my_ang + step, n_ang)).start()
        return carry

    lax.fori_loop(1, n_ang, frac_start, 0)

    k2 = out1 * ch
    pick2 = jnp.where((iota((ch, k2), 1) & (ch - 1)) == iota((ch, k2), 0), 0.5, 0.0).astype(BF16)
    ang2, _ = split(iota((ch, k2), 1), ch, out1)
    all2 = dot(mw[...].reshape(9 * ch, ch), pick2)
    for j in range(3):
        tiles2 = [all2[(i * 3 + j) * ch : (i * 3 + j + 1) * ch] for i in range(3)]
        for a in range(out2):
            block = jnp.zeros((ch, k2), F32)
            for i in range(3):
                block = jnp.where(ang2 == a + i, tiles2[i], block)
            w2[pl.ds(a * ch, ch), pl.ds(j * k2, k2)] = block.astype(BF16)

    bias2 = jnp.concatenate([as_column(mb[...]) * 0.5] * out2, axis=0)

    used = 3 * wide * rows
    x1[pl.ds(per - 8, 8), :] = jnp.where(iota((8, cols), 0) + per - 8 < used + 3, 1.0, 0.0)
    for c, ref in enumerate((dual, forward, sino)):
        for a in range(angs):
            x1[pl.ds((c * wide + 3 + a) * rows, rows), :] = ref[a].astype(F32)
    for copy in halo_copies:
        copy.wait()
    for c in range(3):
        for a in range(3):
            x1[pl.ds((c * wide + a) * rows, rows), :] = halo[0, c, a].astype(F32)
            x1[pl.ds((c * wide + 3 + angs + a) * rows, rows), :] = halo[1, c, a].astype(F32)
    middle = x1[...].astype(BF16)
    store_shifted(x1s, 0, 2 * per, per, middle)
    x1s[pl.ds(per, per), :] = middle
    tiles = cols // TILE

    def layer1(t, carry):
        start = pl.multiple_of(t * TILE, TILE)
        value = silu_of_half(dot(w1[...], x1s[:, pl.ds(start, TILE)])).astype(BF16)
        before = pltpu.roll(value, 1, 1)
        after = pltpu.roll(value, TILE - 1, 1)
        for r in range(rows):
            for j, whole in enumerate((before, value, after)):
                x2[pl.ds((r * 3 + j) * k2, k2), pl.ds(start, TILE)] = whole[r * k2 : (r + 1) * k2]
        return carry

    lax.fori_loop(0, tiles, layer1, 0)

    edge = iota((k2, 128), 1)
    zero = jnp.zeros((k2, 128), BF16)
    for r in range(rows):
        low, mid, high = [pl.ds((r * 3 + j) * k2, k2) for j in range(3)]
        for t in range(tiles):
            first, last = pl.ds(t * TILE, 128), pl.ds((t + 1) * TILE - 128, 128)
            beyond = zero
            if t > 0:
                beyond = pltpu.roll(x2[mid, pl.ds(t * TILE - 128, 128)], 1, 1)
            x2[low, first] = jnp.where(edge == 0, beyond, x2[low, first])
            beyond = zero
            if t < tiles - 1:
                beyond = pltpu.roll(x2[mid, pl.ds((t + 1) * TILE, 128)], 127, 1)
            x2[high, last] = jnp.where(edge == 127, beyond, x2[high, last])

    ramps = 2 * narrow // tiles

    def layer2(t, carry):
        start = pl.multiple_of(t * TILE, TILE)
        for r in range(rows):
            value = dot(w2[...], x2[pl.ds(r * 3 * k2, 3 * k2), pl.ds(start, TILE)]) + bias2
            x3[pl.ds(r * out2 * ch, out2 * ch), pl.ds(start, TILE)] = silu_of_half(value).astype(BF16)
        for n in range(ramps):
            ramp_block(t * ramps + n)
        return carry

    lax.fori_loop(0, tiles, layer2, 0)

    taps = dot(w3[...], x3[...])
    column = iota((ar, cols), 1)
    before = jnp.where(column == 0, 0.0, pltpu.roll(taps[0:ar], 1, 1))
    after = jnp.where(column == cols - 1, 0.0, pltpu.roll(taps[2 * ar : 3 * ar], cols - 1, 1))
    update = before + taps[ar : 2 * ar] + after
    own = x1[pl.ds(3 * rows, ar), :]
    new_dual = (own + update).astype(BF16).astype(F32)
    for a in range(angs):
        nd_out[a] = new_dual[a * rows : (a + 1) * rows].astype(BF16)

    pieces = jnp.concatenate(
        [new_dual[:, n * 128 : (n + 1) * 128] for n in range(narrow)], axis=0
    ).astype(BF16)
    lanes = [None] * narrow
    for pair in range(0, 2 * narrow - 1, 2):
        near = min(2, 2 * narrow - 1 - pair)
        product = dot(pieces, ramp[:, pl.ds(pair * 128, near * 128)])
        for b in range(pair, pair + near):
            for source in range(narrow):
                goal = source + b - (narrow - 1)
                if 0 <= goal < narrow:
                    at = (b - pair) * 128
                    part = product[source * ar : (source + 1) * ar, at : at + 128]
                    lanes[goal] = part if lanes[goal] is None else lanes[goal] + part

    centre = (cols - 1) / 2.0
    mags = by_row(mag, (ar, 128), angs)
    shifts = by_row(shift, (ar, 128), angs)
    halves = cols // n_ang // 128
    size = halves * ar

    def block_copy(source, ang, row):
        return pltpu.make_async_remote_copy(
            src_ref=sent.at[ang],
            dst_ref=got.at[source],
            send_sem=send_sem,
            recv_sem=recv_sem,
            device_id=(ang, row),
            device_id_type=MESH,
        )

    projected = []
    for n in range(cols // 128):
        edges = [
            (x - centre) * m + centre + s
            for x in (n * 128, n * 128 + 127)
            for m in (MAG_LOW, MAG_HIGH)
            for s in (-SHIFT_MAX, SHIFT_MAX)
        ]
        lowest = max(int((min(edges) - 0.1) // 128), 0)
        highest = min(int((max(edges) + 1.1) // 128), cols // 128 - 1)
        places = ((iota((ar, 128), 1) + n * 128).astype(F32) - centre) * mags + centre + shifts
        floors = jnp.floor(places)
        weight = places - floors
        low = floors.astype(jnp.int32)
        ends = []
        for index in (low, low + 1):
            value = jnp.zeros((ar, 128), F32)
            for k in range(lowest, highest + 1):
                taken = jnp.take_along_axis(lanes[k], index & 127, axis=1)
                value = jnp.where(index >> 7 == k, taken, value)
            ends.append(value)
        projected.append((1.0 - weight) * ends[0] + weight * ends[1])
        if len(projected) == halves:
            p = n // halves
            sent[p] = jnp.concatenate(projected, axis=0).astype(BF16)
            projected = []
            for step in range(1, n_row):
                row = lax.rem(my_row + step, n_row)
                block_copy(me, p, row).start()

            @pl.when(my_ang != p)
            def _():
                block_copy(me, p, my_row).start()


    got[me] = sent[my_ang]

    def frac_wait(step, carry):
        peer = lax.rem(my_ang + step, n_ang)
        frac_copy(peer, peer).wait()
        return carry

    lax.fori_loop(1, n_ang, frac_wait, 0)

    slots = order.shape[0] // n_row
    depth = total * size
    zs = slots * SLAB_Z
    place = iota((zs, depth), 1)
    level = iota((zs, depth), 0)
    source_ang = (place >> log2(n_row * size))
    piece_row = ((place >> log2(size)) & (n_row - 1)) * rows + (place & (rows - 1))
    half_of = ((place & (size - 1)) >> log2(ar))
    starts = jnp.zeros((zs, depth), jnp.int32)
    fraction = jnp.zeros((zs, depth), F32)
    for p in range(n_ang):
        here = source_ang == p
        spread = jnp.concatenate([frac_all[p][0:1]] * (depth // 128), axis=1)
        fraction = jnp.where(here, jnp.broadcast_to(spread, (zs, depth)), fraction)
        for k in range(slots):
            first = offsets[p, order[my_row * slots + k]]
            starts = jnp.where(here & ((level >> log2(SLAB_Z)) == k), first, starts)
    reach = piece_row - starts - (level & (SLAB_Z - 1))
    weights = jnp.where(reach == 0, 1.0 - fraction, jnp.where(reach == 1, fraction, 0.0))
    parts = []
    for h in range(halves):
        left_over = jnp.where(half_of == h, weights, 0.0)
        for _ in range(3):
            part = left_over.astype(BF16)
            left_over = left_over - part.astype(F32)
            parts.append(part)
    stacked = jnp.concatenate(parts, axis=0)

    others = got.at[pl.ds(0, total - 1)]
    pltpu.make_async_copy(others, others, recv_sem).wait()

    sums = dot(stacked, got[...].reshape(depth, 128))
    for h in range(halves):
        three = [sums[(h * 3 + s) * zs : (h * 3 + s + 1) * zs] for s in range(3)]
        vol_out[:, pl.ds(h * 128, 128)] = (three[2] + three[1] + three[0]) / math.sqrt(n_ang * angs)
    pltpu.make_async_copy(others, others, send_sem).wait()


def per_device(
    n_ang, n_row, dual_field, forward, sinogram, first_weight, first_bias, middle_weight,
    middle_bias, last_weight, magnify, detector_shift, row_fraction, offsets, slab_order,
):
    angs, rows, cols = dual_field.shape
    ch = first_weight.shape[2]
    operands = (
        dual_field, forward, sinogram, first_weight.transpose(0, 1, 3, 2), first_bias[None, :],
        middle_weight, middle_bias[None, :], last_weight.transpose(0, 2, 1, 3), magnify,
        detector_shift, row_fraction, offsets, slab_order,
    )
    total = n_ang * n_row
    ar = angs * rows
    out1, out2 = angs + 4, angs + 2
    narrow = cols // 128
    width = cols // n_ang
    size = width // 128 * ar
    slots = slab_order.shape[0] // n_row
    vmem = pl.BlockSpec(memory_space=pltpu.VMEM)
    dma = pltpu.SemaphoreType.DMA
    results = pl.pallas_call(
        functools.partial(kernel, n_ang, n_row),
        out_shape=(
            pltpu.VMEM(dual_field.shape, BF16),
            pltpu.VMEM((slots * SLAB_Z, width), F32),
        ),
        in_specs=[pl.BlockSpec(memory_space=pltpu.HBM)] * 13,
        out_specs=(vmem, vmem),
        scratch_shapes=[pltpu.VMEM(x.shape, x.dtype) for x in operands[:8]]
        + [pltpu.SMEM(x.shape, x.dtype) for x in operands[8:]]
        + [
            pltpu.VMEM((2, 3, 3, rows, cols), BF16),
            pltpu.VMEM((64, cols), F32),
            pltpu.VMEM((3 * 64, cols), BF16),
            pltpu.VMEM((rows * 3 * out1 * ch, cols), BF16),
            pltpu.VMEM((rows * out2 * ch, cols), BF16),
            pltpu.VMEM((32, ch), F32),
            pltpu.VMEM((rows * out1 * ch, 3 * 64), BF16),
            pltpu.VMEM((out2 * ch, 3 * out1 * ch), BF16),
            pltpu.VMEM((4 * ar, rows * out2 * ch), BF16),
            pltpu.VMEM((128, 2 * narrow * 128), BF16),
            pltpu.VMEM((8, 128), F32),
            pltpu.VMEM((n_ang, 8, 128), F32),
            pltpu.VMEM((n_ang, size, 128), BF16),
            pltpu.VMEM((total, size, 128), BF16),
            dma((2, 3)),
            dma((2, 3)),
            dma((n_ang,)),
            dma((n_ang,)),
            dma(()),
            dma(()),
            dma((13,)),
        ],
        compiler_params=pltpu.CompilerParams(
            collective_id=0, has_side_effects=True, vmem_limit_bytes=65280 * 1024
        ),
        cost_estimate=pl.CostEstimate(flops=10**9, bytes_accessed=10**6, transcendentals=0),
    )(*operands)
    hbm = pl.BlockSpec(memory_space=pltpu.HBM)
    return pl.pallas_call(
        write_out,
        out_shape=tuple(jax.ShapeDtypeStruct(x.shape, x.dtype) for x in results),
        in_specs=[vmem, vmem],
        out_specs=(hbm, hbm),
        scratch_shapes=[dma((2,))],
    )(*results)


def write_out(nd_in, vol_in, nd_out, vol_out, sems):
    first = pltpu.make_async_copy(nd_in, nd_out, sems.at[0])
    second = pltpu.make_async_copy(vol_in, vol_out, sems.at[1])
    first.start()
    second.start()
    first.wait()
    second.wait()


def solution(mesh):
    sizes = dict(mesh.shape)
    split = P("ang", "row", None)
    return jax.shard_map(
        functools.partial(per_device, sizes["ang"], sizes["row"]),
        mesh=mesh,
        in_specs=(
            split, split, split, P(), P(), P(), P(), P(), P("ang"), P("ang"), P("ang"), P(), P(),
        ),
        out_specs=(split, P("row", "ang")),
        check_vma=False,
    )
```

```python
import functools
import math

import jax
import jax.numpy as jnp
from jax import lax
from jax.experimental import pallas as pl
from jax.experimental.pallas import tpu as pltpu
from jax.sharding import PartitionSpec as P

SLAB_Z = 4
MAG_LOW, MAG_HIGH, SHIFT_MAX = 0.85, 0.95, 8.0
TILE = 512
F32 = jnp.float32
BF16 = jnp.bfloat16
MESH = pl.DeviceIdType.MESH


def dot(a, b):
    return jnp.dot(a, b, preferred_element_type=F32)


def silu_of_half(half):
    return half + half * jnp.tanh(half)


def iota(shape, dim):
    return lax.broadcasted_iota(jnp.int32, shape, dim)


def as_column(row):
    size = row.shape[1]
    spread = jnp.broadcast_to(row, (size, size))
    return jnp.sum(
        jnp.where(iota((size, size), 0) == iota((size, size), 1), spread, 0.0), axis=1, keepdims=True
    )


def by_row(ref, shape, period):
    index = iota(shape, 0) // 2
    value = jnp.full(shape, ref[0], F32)
    for a in range(1, period):
        value = jnp.where(index == a, ref[a], value)
    return value


def log2(size):
    assert size & (size - 1) == 0
    return size.bit_length() - 1


def split(value, size, count):
    quotient = jnp.zeros_like(value)
    for k in range(1, count):
        quotient = quotient + jnp.where(value >= k * size, 1, 0)
    return quotient, value - quotient * size


def store_shifted(ref, first_before, first_after, count, values):
    cols = values.shape[1]
    column = iota((count, 128), 1)
    zero = jnp.zeros((count, 128), values.dtype)
    before = pltpu.roll(values, 1, 1)
    after = pltpu.roll(values, cols - 1, 1)
    ref[pl.ds(first_before, count), pl.ds(128, cols - 128)] = before[:, 128:]
    ref[pl.ds(first_before, count), pl.ds(0, 128)] = jnp.where(column == 0, zero, before[:, :128])
    ref[pl.ds(first_after, count), pl.ds(0, cols - 128)] = after[:, : cols - 128]
    ref[pl.ds(first_after, count), pl.ds(cols - 128, 128)] = jnp.where(
        column == 127, zero, after[:, cols - 128 :]
    )


def kernel(
    n_ang, n_row, *refs,
):
    sources, (nd_out, vol_out), locals_ = refs[:13], refs[13:15], refs[15:28]
    dual, forward, sino, fw, fb, mw, mb, lw, mag, shift, frac, offsets, order = locals_
    (
    halo, x1, x1s, x2, x3, wrows, w1, w2, w3, ramp, frac_own, frac_all, sent, got,
    halo_send, halo_recv, frac_send, frac_recv, send_sem, recv_sem, local_sem,
    ) = refs[28:]
    loads = [
        pltpu.make_async_copy(source, goal, local_sem.at[n])
        for n, (source, goal) in enumerate(zip(sources, locals_))
    ]
    angs, rows, cols = dual.shape
    ch = mw.shape[2]
    total = n_ang * n_row
    my_ang, my_row = lax.axis_index("ang"), lax.axis_index("row")
    me = my_ang * n_row + my_row
    wide = angs + 6
    out1, out2 = angs + 4, angs + 2
    ar = angs * rows
    per = 64

    def place_of(step):
        target = lax.rem(me + step, total)
        return target, target // n_row, lax.rem(target, n_row)

    barrier = pltpu.get_barrier_semaphore()

    def greet(step, carry):
        _, ang, row = place_of(step)
        pl.semaphore_signal(barrier, inc=1, device_id=(ang, row), device_id_type=MESH)
        return carry

    lax.fori_loop(1, total, greet, 0)
    for load in loads:
        load.start()

    narrow = cols // 128

    def ramp_block(b):
        away = (b - (narrow - 1)) * 128 + iota((128, 128), 1) - iota((128, 128), 0)
        odd = (away & 1) == 1
        distance = jnp.where(odd, away, 1).astype(F32)
        value = jnp.where(odd, -1.0 / (math.pi * math.pi * distance * distance), 0.0)
        ramp[:, pl.ds(pl.multiple_of(b * 128, 128), 128)] = jnp.where(away == 0, 0.25, value).astype(BF16)

    for load in loads:
        load.wait()
    k1 = 3 * per
    tap1, rest1 = split(iota((ch, k1), 1), per, 3)
    chan1, rest1 = split(rest1, wide * rows, 4)
    ang1 = jnp.where(chan1 < 3, rest1 >> 1, -9)
    row1 = rest1 & 1
    for i in range(3):
        for j in range(3):
            wrows[pl.ds((i * 3 + j) * 3, 3), :] = fw[i, j].astype(F32)
    entry = iota((32, 4 * per), 0)
    tap_all, rest_all = split(iota((32, 4 * per), 1), per, 4)
    chan_all, _ = split(rest_all, wide * rows, 4)
    chosen = jnp.where(chan_all < 3, tap_all * 3 + chan_all, -99)
    chosen = jnp.where(tap_all < 3, chosen, -99)
    pick1 = jnp.concatenate(
        [jnp.where(entry == chosen + i * 9, 0.5, 0.0).astype(BF16) for i in range(3)], axis=1
    )
    entries = jnp.where(iota((32, ch), 0) < 27, wrows[...], 0.0).astype(BF16)
    tiles1 = lax.dot_general(entries, pick1, (((0,), (0,)), ((), ())), preferred_element_type=F32)
    joined1 = [tiles1[:, i * 4 * per : i * 4 * per + k1] for i in range(3)]
    bias1 = jnp.zeros((ch, k1), F32)
    left_over = as_column(fb[...]) * 0.5
    for n in range(3):
        part = left_over.astype(BF16).astype(F32)
        left_over = left_over - part
        bias1 = jnp.where(iota((ch, k1), 1) == per + 3 * wide * rows + n, part, bias1)
    for r in range(rows):
        for a in range(out1):
            block = bias1
            for i in range(3):
                block = jnp.where((ang1 == a + i) & (row1 == r), joined1[i], block)
            w1[pl.ds((r * out1 + a) * ch, ch), :] = block.astype(BF16)

    k3 = rows * out2 * ch
    pick3 = jnp.where((iota((ch, k3), 1) & (ch - 1)) == iota((ch, k3), 0), 1.0, 0.0).astype(BF16)
    row3, rest3 = split(iota((ar, k3), 1), out2 * ch, rows)
    ang3, _ = split(rest3, ch, out2)
    ang3 = ang3 - (iota((ar, k3), 0) >> 1)
    same3 = row3 == (iota((ar, k3), 0) & 1)
    spread3 = [
        jnp.broadcast_to(lw[i, 0, j : j + 1, :].astype(F32), (ar, ch)) for i in range(3) for j in range(3)
    ]
    all3 = dot(jnp.concatenate(spread3, axis=0).astype(BF16), pick3)
    blocks3 = []
    for j in range(3):
        block = jnp.zeros((ar, k3), F32)
        for i in range(3):
            at = (i * 3 + j) * ar
            block = jnp.where((ang3 == i) & same3, all3[at : at + ar], block)
        blocks3.append(block)
    blocks3.append(jnp.zeros((ar, k3), F32))
    w3[...] = jnp.concatenate(blocks3, axis=0).astype(BF16)

    pl.semaphore_wait(barrier, total - 1)

    left = lax.rem(my_ang + n_ang - 1, n_ang)
    right = lax.rem(my_ang + 1, n_ang)
    halo_copies = []
    for c, ref in enumerate(sources[:3]):
        for side, (peer, first) in enumerate(((right, angs - 3), (left, 0))):
            copy = pltpu.make_async_remote_copy(
                src_ref=ref.at[pl.ds(first, 3)],
                dst_ref=halo.at[side, c],
                send_sem=halo_send.at[side, c],
                recv_sem=halo_recv.at[side, c],
                device_id=(peer, my_row),
                device_id_type=MESH,
            )
            copy.start()
            halo_copies.append(copy)

    lane = iota((8, 128), 1)
    mine = jnp.full((8, 128), frac[0], F32)
    for a in range(1, angs):
        mine = jnp.where((lane & (ar - 1)) // rows == a, frac[a], mine)
    frac_own[...] = mine
    frac_all[my_ang] = mine

    def frac_copy(source, target):
        return pltpu.make_async_remote_copy(
            src_ref=frac_own,
            dst_ref=frac_all.at[source],
            send_sem=frac_send.at[target],
            recv_sem=frac_recv.at[source],
            device_id=(target, my_row),
            device_id_type=MESH,
        )

    def frac_start(step, carry):
        frac_copy(my_ang, lax.rem(my_ang + step, n_ang)).start()
        return carry

    lax.fori_loop(1, n_ang, frac_start, 0)

    k2 = out1 * ch
    pick2 = jnp.where((iota((ch, k2), 1) & (ch - 1)) == iota((ch, k2), 0), 0.5, 0.0).astype(BF16)
    ang2, _ = split(iota((ch, k2), 1), ch, out1)
    all2 = dot(mw[...].reshape(9 * ch, ch), pick2)
    for j in range(3):
        tiles2 = [all2[(i * 3 + j) * ch : (i * 3 + j + 1) * ch] for i in range(3)]
        for a in range(out2):
            block = jnp.zeros((ch, k2), F32)
            for i in range(3):
                block = jnp.where(ang2 == a + i, tiles2[i], block)
            w2[pl.ds(a * ch, ch), pl.ds(j * k2, k2)] = block.astype(BF16)

    bias2 = jnp.concatenate([as_column(mb[...]) * 0.5] * out2, axis=0)

    used = 3 * wide * rows
    x1[pl.ds(per - 8, 8), :] = jnp.where(iota((8, cols), 0) + per - 8 < used + 3, 1.0, 0.0)
    for c, ref in enumerate((dual, forward, sino)):
        for a in range(angs):
            x1[pl.ds((c * wide + 3 + a) * rows, rows), :] = ref[a].astype(F32)
    for copy in halo_copies:
        copy.wait()
    for c in range(3):
        for a in range(3):
            x1[pl.ds((c * wide + a) * rows, rows), :] = halo[0, c, a].astype(F32)
            x1[pl.ds((c * wide + 3 + angs + a) * rows, rows), :] = halo[1, c, a].astype(F32)
    middle = x1[...].astype(BF16)
    store_shifted(x1s, 0, 2 * per, per, middle)
    x1s[pl.ds(per, per), :] = middle
    tiles = cols // TILE

    def layer1(t, carry):
        start = pl.multiple_of(t * TILE, TILE)
        value = silu_of_half(dot(w1[...], x1s[:, pl.ds(start, TILE)])).astype(BF16)
        before = pltpu.roll(value, 1, 1)
        after = pltpu.roll(value, TILE - 1, 1)
        for r in range(rows):
            for j, whole in enumerate((before, value, after)):
                x2[pl.ds((r * 3 + j) * k2, k2), pl.ds(start, TILE)] = whole[r * k2 : (r + 1) * k2]
        return carry

    lax.fori_loop(0, tiles, layer1, 0)

    edge = iota((k2, 128), 1)
    zero = jnp.zeros((k2, 128), BF16)
    for r in range(rows):
        low, mid, high = [pl.ds((r * 3 + j) * k2, k2) for j in range(3)]
        for t in range(tiles):
            first, last = pl.ds(t * TILE, 128), pl.ds((t + 1) * TILE - 128, 128)
            beyond = zero
            if t > 0:
                beyond = pltpu.roll(x2[mid, pl.ds(t * TILE - 128, 128)], 1, 1)
            x2[low, first] = jnp.where(edge == 0, beyond, x2[low, first])
            beyond = zero
            if t < tiles - 1:
                beyond = pltpu.roll(x2[mid, pl.ds((t + 1) * TILE, 128)], 127, 1)
            x2[high, last] = jnp.where(edge == 127, beyond, x2[high, last])

    ramps = 2 * narrow // tiles

    def layer2(t, carry):
        start = pl.multiple_of(t * TILE, TILE)
        for r in range(rows):
            value = dot(w2[...], x2[pl.ds(r * 3 * k2, 3 * k2), pl.ds(start, TILE)]) + bias2
            x3[pl.ds(r * out2 * ch, out2 * ch), pl.ds(start, TILE)] = silu_of_half(value).astype(BF16)
        for n in range(ramps):
            ramp_block(t * ramps + n)
        return carry

    lax.fori_loop(0, tiles, layer2, 0)

    taps = dot(w3[...], x3[...])
    column = iota((ar, cols), 1)
    before = jnp.where(column == 0, 0.0, pltpu.roll(taps[0:ar], 1, 1))
    after = jnp.where(column == cols - 1, 0.0, pltpu.roll(taps[2 * ar : 3 * ar], cols - 1, 1))
    update = before + taps[ar : 2 * ar] + after
    own = x1[pl.ds(3 * rows, ar), :]
    new_dual = (own + update).astype(BF16).astype(F32)
    for a in range(angs):
        nd_out[a] = new_dual[a * rows : (a + 1) * rows].astype(BF16)

    pieces = jnp.concatenate(
        [new_dual[:, n * 128 : (n + 1) * 128] for n in range(narrow)], axis=0
    ).astype(BF16)
    lanes = [None] * narrow
    for pair in range(0, 2 * narrow - 1, 2):
        near = min(2, 2 * narrow - 1 - pair)
        product = dot(pieces, ramp[:, pl.ds(pair * 128, near * 128)])
        for b in range(pair, pair + near):
            for source in range(narrow):
                goal = source + b - (narrow - 1)
                if 0 <= goal < narrow:
                    at = (b - pair) * 128
                    part = product[source * ar : (source + 1) * ar, at : at + 128]
                    lanes[goal] = part if lanes[goal] is None else lanes[goal] + part

    centre = (cols - 1) / 2.0
    mags = by_row(mag, (ar, 128), angs)
    shifts = by_row(shift, (ar, 128), angs)
    halves = cols // n_ang // 128
    size = halves * ar

    def block_copy(source, ang, row):
        return pltpu.make_async_remote_copy(
            src_ref=sent.at[ang],
            dst_ref=got.at[source],
            send_sem=send_sem,
            recv_sem=recv_sem,
            device_id=(ang, row),
            device_id_type=MESH,
        )

    projected = []
    for n in range(cols // 128):
        edges = [
            (x - centre) * m + centre + s
            for x in (n * 128, n * 128 + 127)
            for m in (MAG_LOW, MAG_HIGH)
            for s in (-SHIFT_MAX, SHIFT_MAX)
        ]
        lowest = max(int((min(edges) - 0.1) // 128), 0)
        highest = min(int((max(edges) + 1.1) // 128), cols // 128 - 1)
        places = ((iota((ar, 128), 1) + n * 128).astype(F32) - centre) * mags + centre + shifts
        floors = jnp.floor(places)
        weight = places - floors
        low = floors.astype(jnp.int32)
        ends = []
        for index in (low, low + 1):
            value = jnp.zeros((ar, 128), F32)
            for k in range(lowest, highest + 1):
                taken = jnp.take_along_axis(lanes[k], index & 127, axis=1)
                value = jnp.where(index >> 7 == k, taken, value)
            ends.append(value)
        projected.append((1.0 - weight) * ends[0] + weight * ends[1])
        if len(projected) == halves:
            p = n // halves
            sent[p] = jnp.concatenate(projected, axis=0).astype(BF16)
            projected = []
            for step in range(1, n_row):
                row = lax.rem(my_row + step, n_row)
                block_copy(me, p, row).start()

            @pl.when(my_ang != p)
            def _():
                block_copy(me, p, my_row).start()


    got[me] = sent[my_ang]

    def frac_wait(step, carry):
        peer = lax.rem(my_ang + step, n_ang)
        frac_copy(peer, peer).wait()
        return carry

    lax.fori_loop(1, n_ang, frac_wait, 0)

    slots = order.shape[0] // n_row
    depth = total * size
    zs = slots * SLAB_Z
    place = iota((zs, depth), 1)
    level = iota((zs, depth), 0)
    source_ang = (place >> log2(n_row * size))
    piece_row = ((place >> log2(size)) & (n_row - 1)) * rows + (place & (rows - 1))
    half_of = ((place & (size - 1)) >> log2(ar))
    starts = jnp.zeros((zs, depth), jnp.int32)
    fraction = jnp.zeros((zs, depth), F32)
    for p in range(n_ang):
        here = source_ang == p
        spread = jnp.concatenate([frac_all[p][0:1]] * (depth // 128), axis=1)
        fraction = jnp.where(here, jnp.broadcast_to(spread, (zs, depth)), fraction)
        for k in range(slots):
            first = offsets[p, order[my_row * slots + k]]
            starts = jnp.where(here & ((level >> log2(SLAB_Z)) == k), first, starts)
    reach = piece_row - starts - (level & (SLAB_Z - 1))
    weights = jnp.where(reach == 0, 1.0 - fraction, jnp.where(reach == 1, fraction, 0.0))
    parts = []
    for h in range(halves):
        left_over = jnp.where(half_of == h, weights, 0.0)
        for _ in range(3):
            part = left_over.astype(BF16)
            left_over = left_over - part.astype(F32)
            parts.append(part)
    stacked = jnp.concatenate(parts, axis=0)

    others = got.at[pl.ds(0, total - 1)]
    pltpu.make_async_copy(others, others, recv_sem).wait()

    sums = dot(stacked, got[...].reshape(depth, 128))
    for h in range(halves):
        three = [sums[(h * 3 + s) * zs : (h * 3 + s + 1) * zs] for s in range(3)]
        vol_out[:, pl.ds(h * 128, 128)] = (three[2] + three[1] + three[0]) / math.sqrt(n_ang * angs)
    pltpu.make_async_copy(others, others, send_sem).wait()


def per_device(
    n_ang, n_row, dual_field, forward, sinogram, first_weight, first_bias, middle_weight,
    middle_bias, last_weight, magnify, detector_shift, row_fraction, offsets, slab_order,
):
    angs, rows, cols = dual_field.shape
    ch = first_weight.shape[2]
    operands = (
        dual_field, forward, sinogram, first_weight.transpose(0, 1, 3, 2), first_bias[None, :],
        middle_weight, middle_bias[None, :], last_weight.transpose(0, 2, 1, 3), magnify,
        detector_shift, row_fraction, offsets, slab_order,
    )
    total = n_ang * n_row
    ar = angs * rows
    out1, out2 = angs + 4, angs + 2
    narrow = cols // 128
    width = cols // n_ang
    size = width // 128 * ar
    slots = slab_order.shape[0] // n_row
    vmem = pl.BlockSpec(memory_space=pltpu.VMEM)
    dma = pltpu.SemaphoreType.DMA
    return pl.pallas_call(
        functools.partial(kernel, n_ang, n_row),
        out_shape=(
            pltpu.VMEM(dual_field.shape, BF16),
            pltpu.VMEM((slots * SLAB_Z, width), F32),
        ),
        in_specs=[pl.BlockSpec(memory_space=pltpu.HBM)] * 13,
        out_specs=(vmem, vmem),
        scratch_shapes=[pltpu.VMEM(x.shape, x.dtype) for x in operands[:8]]
        + [pltpu.SMEM(x.shape, x.dtype) for x in operands[8:]]
        + [
            pltpu.VMEM((2, 3, 3, rows, cols), BF16),
            pltpu.VMEM((64, cols), F32),
            pltpu.VMEM((3 * 64, cols), BF16),
            pltpu.VMEM((rows * 3 * out1 * ch, cols), BF16),
            pltpu.VMEM((rows * out2 * ch, cols), BF16),
            pltpu.VMEM((32, ch), F32),
            pltpu.VMEM((rows * out1 * ch, 3 * 64), BF16),
            pltpu.VMEM((out2 * ch, 3 * out1 * ch), BF16),
            pltpu.VMEM((4 * ar, rows * out2 * ch), BF16),
            pltpu.VMEM((128, 2 * narrow * 128), BF16),
            pltpu.VMEM((8, 128), F32),
            pltpu.VMEM((n_ang, 8, 128), F32),
            pltpu.VMEM((n_ang, size, 128), BF16),
            pltpu.VMEM((total, size, 128), BF16),
            dma((2, 3)),
            dma((2, 3)),
            dma((n_ang,)),
            dma((n_ang,)),
            dma(()),
            dma(()),
            dma((13,)),
        ],
        compiler_params=pltpu.CompilerParams(
            collective_id=0, has_side_effects=True, vmem_limit_bytes=65280 * 1024
        ),
        cost_estimate=pl.CostEstimate(flops=10**9, bytes_accessed=10**6, transcendentals=0),
    )(*operands)


def solution(mesh):
    sizes = dict(mesh.shape)
    split = P("ang", "row", None)
    return jax.shard_map(
        functools.partial(per_device, sizes["ang"], sizes["row"]),
        mesh=mesh,
        in_specs=(
            split, split, split, P(), P(), P(), P(), P(), P("ang"), P("ang"), P("ang"), P(), P(),
        ),
        out_specs=(split, P("row", "ang")),
        check_vma=False,
    )
```

```python
import functools
import math

import jax
import jax.numpy as jnp
from jax import lax
from jax.experimental import pallas as pl
from jax.experimental.pallas import tpu as pltpu
from jax.sharding import PartitionSpec as P

SLAB_Z = 4
MAG_LOW, MAG_HIGH, SHIFT_MAX = 0.85, 0.95, 8.0
TILE = 512
F32 = jnp.float32
BF16 = jnp.bfloat16
MESH = pl.DeviceIdType.MESH


def dot(a, b):
    return jnp.dot(a, b, preferred_element_type=F32)


def silu_of_half(half):
    return half + half * jnp.tanh(half)


def iota(shape, dim):
    return lax.broadcasted_iota(jnp.int32, shape, dim)


def as_column(row):
    size = row.shape[1]
    spread = jnp.broadcast_to(row, (size, size))
    return jnp.sum(
        jnp.where(iota((size, size), 0) == iota((size, size), 1), spread, 0.0), axis=1, keepdims=True
    )


def by_row(ref, shape, period):
    index = iota(shape, 0) // 2
    value = jnp.full(shape, ref[0], F32)
    for a in range(1, period):
        value = jnp.where(index == a, ref[a], value)
    return value


def log2(size):
    assert size & (size - 1) == 0
    return size.bit_length() - 1


def split(value, size, count):
    quotient = jnp.zeros_like(value)
    for k in range(1, count):
        quotient = quotient + jnp.where(value >= k * size, 1, 0)
    return quotient, value - quotient * size


def store_shifted(ref, first_before, first_after, count, values):
    cols = values.shape[1]
    column = iota((count, 128), 1)
    zero = jnp.zeros((count, 128), values.dtype)
    before = pltpu.roll(values, 1, 1)
    after = pltpu.roll(values, cols - 1, 1)
    ref[pl.ds(first_before, count), pl.ds(128, cols - 128)] = before[:, 128:]
    ref[pl.ds(first_before, count), pl.ds(0, 128)] = jnp.where(column == 0, zero, before[:, :128])
    ref[pl.ds(first_after, count), pl.ds(0, cols - 128)] = after[:, : cols - 128]
    ref[pl.ds(first_after, count), pl.ds(cols - 128, 128)] = jnp.where(
        column == 127, zero, after[:, cols - 128 :]
    )


def kernel(
    n_ang, n_row, *refs,
):
    sources, (nd_out, vol_out), locals_ = refs[:13], refs[13:15], refs[15:28]
    dual, forward, sino, fw, fb, mw, mb, lw, mag, shift, frac, offsets, order = locals_
    (
    halo, x1, x1s, x2, x3, wrows, w1, w2, w3, ramp, frac_own, frac_all, sent, got,
    halo_send, halo_recv, frac_send, frac_recv, send_sem, recv_sem, local_sem,
    ) = refs[28:]
    loads = [
        pltpu.make_async_copy(source, goal, local_sem.at[n])
        for n, (source, goal) in enumerate(zip(sources, locals_))
    ]
    angs, rows, cols = dual.shape
    ch = mw.shape[2]
    total = n_ang * n_row
    my_ang, my_row = lax.axis_index("ang"), lax.axis_index("row")
    me = my_ang * n_row + my_row
    wide = angs + 6
    out1, out2 = angs + 4, angs + 2
    ar = angs * rows
    per = 64

    def place_of(step):
        target = lax.rem(me + step, total)
        return target, target // n_row, lax.rem(target, n_row)

    barrier = pltpu.get_barrier_semaphore()

    def greet(step, carry):
        _, ang, row = place_of(step)
        pl.semaphore_signal(barrier, inc=1, device_id=(ang, row), device_id_type=MESH)
        return carry

    lax.fori_loop(1, total, greet, 0)
    for load in loads:
        load.start()

    narrow = cols // 128

    def ramp_block(b):
        away = (b - (narrow - 1)) * 128 + iota((128, 128), 1) - iota((128, 128), 0)
        odd = (away & 1) == 1
        distance = jnp.where(odd, away, 1).astype(F32)
        value = jnp.where(odd, -1.0 / (math.pi * math.pi * distance * distance), 0.0)
        ramp[:, pl.ds(pl.multiple_of(b * 128, 128), 128)] = jnp.where(away == 0, 0.25, value).astype(BF16)

    for load in loads:
        load.wait()
    k1 = 3 * per
    tap1, rest1 = split(iota((ch, k1), 1), per, 3)
    chan1, rest1 = split(rest1, wide * rows, 4)
    ang1 = jnp.where(chan1 < 3, rest1 >> 1, -9)
    row1 = rest1 & 1
    for i in range(3):
        for j in range(3):
            wrows[pl.ds((i * 3 + j) * 3, 3), :] = fw[i, j].astype(F32)
    entry = iota((32, 4 * per), 0)
    tap_all, rest_all = split(iota((32, 4 * per), 1), per, 4)
    chan_all, _ = split(rest_all, wide * rows, 4)
    chosen = jnp.where(chan_all < 3, tap_all * 3 + chan_all, -99)
    chosen = jnp.where(tap_all < 3, chosen, -99)
    pick1 = jnp.concatenate(
        [jnp.where(entry == chosen + i * 9, 0.5, 0.0).astype(BF16) for i in range(3)], axis=1
    )
    entries = jnp.where(iota((32, ch), 0) < 27, wrows[...], 0.0).astype(BF16)
    tiles1 = lax.dot_general(entries, pick1, (((0,), (0,)), ((), ())), preferred_element_type=F32)
    joined1 = [tiles1[:, i * 4 * per : i * 4 * per + k1] for i in range(3)]
    bias1 = jnp.zeros((ch, k1), F32)
    left_over = as_column(fb[...]) * 0.5
    for n in range(3):
        part = left_over.astype(BF16).astype(F32)
        left_over = left_over - part
        bias1 = jnp.where(iota((ch, k1), 1) == per + 3 * wide * rows + n, part, bias1)
    for r in range(rows):
        for a in range(out1):
            block = bias1
            for i in range(3):
                block = jnp.where((ang1 == a + i) & (row1 == r), joined1[i], block)
            w1[pl.ds((r * out1 + a) * ch, ch), :] = block.astype(BF16)

    k3 = rows * out2 * ch
    pick3 = jnp.where((iota((ch, k3), 1) & (ch - 1)) == iota((ch, k3), 0), 1.0, 0.0).astype(BF16)
    row3, rest3 = split(iota((ar, k3), 1), out2 * ch, rows)
    ang3, _ = split(rest3, ch, out2)
    ang3 = ang3 - (iota((ar, k3), 0) >> 1)
    same3 = row3 == (iota((ar, k3), 0) & 1)
    spread3 = [
        jnp.broadcast_to(lw[i, 0, j : j + 1, :].astype(F32), (ar, ch)) for i in range(3) for j in range(3)
    ]
    all3 = dot(jnp.concatenate(spread3, axis=0).astype(BF16), pick3)
    blocks3 = []
    for j in range(3):
        block = jnp.zeros((ar, k3), F32)
        for i in range(3):
            at = (i * 3 + j) * ar
            block = jnp.where((ang3 == i) & same3, all3[at : at + ar], block)
        blocks3.append(block)
    blocks3.append(jnp.zeros((ar, k3), F32))
    w3[...] = jnp.concatenate(blocks3, axis=0).astype(BF16)

    used = 3 * wide * rows
    x1[pl.ds(per - 8, 8), :] = jnp.where(iota((8, cols), 0) + per - 8 < used + 3, 1.0, 0.0)
    for c, ref in enumerate((dual, forward, sino)):
        for a in range(angs):
            x1[pl.ds((c * wide + 3 + a) * rows, rows), :] = ref[a].astype(F32)
    pl.semaphore_wait(barrier, total - 1)

    left = lax.rem(my_ang + n_ang - 1, n_ang)
    right = lax.rem(my_ang + 1, n_ang)
    halo_copies = []
    for c, ref in enumerate(sources[:3]):
        for side, (peer, first) in enumerate(((right, angs - 3), (left, 0))):
            copy = pltpu.make_async_remote_copy(
                src_ref=ref.at[pl.ds(first, 3)],
                dst_ref=halo.at[side, c],
                send_sem=halo_send.at[side, c],
                recv_sem=halo_recv.at[side, c],
                device_id=(peer, my_row),
                device_id_type=MESH,
            )
            copy.start()
            halo_copies.append(copy)

    lane = iota((8, 128), 1)
    mine = jnp.full((8, 128), frac[0], F32)
    for a in range(1, angs):
        mine = jnp.where((lane & (ar - 1)) // rows == a, frac[a], mine)
    frac_own[...] = mine
    frac_all[my_ang] = mine

    def frac_copy(source, target):
        return pltpu.make_async_remote_copy(
            src_ref=frac_own,
            dst_ref=frac_all.at[source],
            send_sem=frac_send.at[target],
            recv_sem=frac_recv.at[source],
            device_id=(target, my_row),
            device_id_type=MESH,
        )

    def frac_start(step, carry):
        frac_copy(my_ang, lax.rem(my_ang + step, n_ang)).start()
        return carry

    lax.fori_loop(1, n_ang, frac_start, 0)

    k2 = out1 * ch
    pick2 = jnp.where((iota((ch, k2), 1) & (ch - 1)) == iota((ch, k2), 0), 0.5, 0.0).astype(BF16)
    ang2, _ = split(iota((ch, k2), 1), ch, out1)
    all2 = dot(mw[...].reshape(9 * ch, ch), pick2)
    for j in range(3):
        tiles2 = [all2[(i * 3 + j) * ch : (i * 3 + j + 1) * ch] for i in range(3)]
        for a in range(out2):
            block = jnp.zeros((ch, k2), F32)
            for i in range(3):
                block = jnp.where(ang2 == a + i, tiles2[i], block)
            w2[pl.ds(a * ch, ch), pl.ds(j * k2, k2)] = block.astype(BF16)

    bias2 = jnp.concatenate([as_column(mb[...]) * 0.5] * out2, axis=0)

    for copy in halo_copies:
        copy.wait_recv()
    for c in range(3):
        for a in range(3):
            x1[pl.ds((c * wide + a) * rows, rows), :] = halo[0, c, a].astype(F32)
            x1[pl.ds((c * wide + 3 + angs + a) * rows, rows), :] = halo[1, c, a].astype(F32)
    middle = x1[...].astype(BF16)
    store_shifted(x1s, 0, 2 * per, per, middle)
    x1s[pl.ds(per, per), :] = middle
    tiles = cols // TILE

    def layer1(t, carry):
        start = pl.multiple_of(t * TILE, TILE)
        value = silu_of_half(dot(w1[...], x1s[:, pl.ds(start, TILE)])).astype(BF16)
        before = pltpu.roll(value, 1, 1)
        after = pltpu.roll(value, TILE - 1, 1)
        for r in range(rows):
            for j, whole in enumerate((before, value, after)):
                x2[pl.ds((r * 3 + j) * k2, k2), pl.ds(start, TILE)] = whole[r * k2 : (r + 1) * k2]
        return carry

    lax.fori_loop(0, tiles, layer1, 0)

    edge = iota((k2, 128), 1)
    zero = jnp.zeros((k2, 128), BF16)
    for r in range(rows):
        low, mid, high = [pl.ds((r * 3 + j) * k2, k2) for j in range(3)]
        for t in range(tiles):
            first, last = pl.ds(t * TILE, 128), pl.ds((t + 1) * TILE - 128, 128)
            beyond = zero
            if t > 0:
                beyond = pltpu.roll(x2[mid, pl.ds(t * TILE - 128, 128)], 1, 1)
            x2[low, first] = jnp.where(edge == 0, beyond, x2[low, first])
            beyond = zero
            if t < tiles - 1:
                beyond = pltpu.roll(x2[mid, pl.ds((t + 1) * TILE, 128)], 127, 1)
            x2[high, last] = jnp.where(edge == 127, beyond, x2[high, last])

    ramps = 2 * narrow // tiles

    def layer2(t, carry):
        start = pl.multiple_of(t * TILE, TILE)
        for r in range(rows):
            value = dot(w2[...], x2[pl.ds(r * 3 * k2, 3 * k2), pl.ds(start, TILE)]) + bias2
            x3[pl.ds(r * out2 * ch, out2 * ch), pl.ds(start, TILE)] = silu_of_half(value).astype(BF16)
        for n in range(ramps):
            ramp_block(t * ramps + n)
        return carry

    lax.fori_loop(0, tiles, layer2, 0)

    taps = dot(w3[...], x3[...])
    column = iota((ar, cols), 1)
    before = jnp.where(column == 0, 0.0, pltpu.roll(taps[0:ar], 1, 1))
    after = jnp.where(column == cols - 1, 0.0, pltpu.roll(taps[2 * ar : 3 * ar], cols - 1, 1))
    update = before + taps[ar : 2 * ar] + after
    own = x1[pl.ds(3 * rows, ar), :]
    new_dual = (own + update).astype(BF16).astype(F32)
    for a in range(angs):
        nd_out[a] = new_dual[a * rows : (a + 1) * rows].astype(BF16)

    pieces = jnp.concatenate(
        [new_dual[:, n * 128 : (n + 1) * 128] for n in range(narrow)], axis=0
    ).astype(BF16)
    lanes = [None] * narrow
    for pair in range(0, 2 * narrow - 1, 2):
        near = min(2, 2 * narrow - 1 - pair)
        product = dot(pieces, ramp[:, pl.ds(pair * 128, near * 128)])
        for b in range(pair, pair + near):
            for source in range(narrow):
                goal = source + b - (narrow - 1)
                if 0 <= goal < narrow:
                    at = (b - pair) * 128
                    part = product[source * ar : (source + 1) * ar, at : at + 128]
                    lanes[goal] = part if lanes[goal] is None else lanes[goal] + part

    centre = (cols - 1) / 2.0
    mags = by_row(mag, (ar, 128), angs)
    shifts = by_row(shift, (ar, 128), angs)
    halves = cols // n_ang // 128
    size = halves * ar

    def block_copy(source, ang, row):
        return pltpu.make_async_remote_copy(
            src_ref=sent.at[ang],
            dst_ref=got.at[source],
            send_sem=send_sem,
            recv_sem=recv_sem,
            device_id=(ang, row),
            device_id_type=MESH,
        )

    projected = []
    for n in range(cols // 128):
        edges = [
            (x - centre) * m + centre + s
            for x in (n * 128, n * 128 + 127)
            for m in (MAG_LOW, MAG_HIGH)
            for s in (-SHIFT_MAX, SHIFT_MAX)
        ]
        lowest = max(int((min(edges) - 0.1) // 128), 0)
        highest = min(int((max(edges) + 1.1) // 128), cols // 128 - 1)
        places = ((iota((ar, 128), 1) + n * 128).astype(F32) - centre) * mags + centre + shifts
        floors = jnp.floor(places)
        weight = places - floors
        low = floors.astype(jnp.int32)
        ends = []
        for index in (low, low + 1):
            value = jnp.zeros((ar, 128), F32)
            for k in range(lowest, highest + 1):
                taken = jnp.take_along_axis(lanes[k], index & 127, axis=1)
                value = jnp.where(index >> 7 == k, taken, value)
            ends.append(value)
        projected.append((1.0 - weight) * ends[0] + weight * ends[1])
        if len(projected) == halves:
            p = n // halves
            sent[p] = jnp.concatenate(projected, axis=0).astype(BF16)
            projected = []
            for step in range(1, n_row):
                row = lax.rem(my_row + step, n_row)
                block_copy(me, p, row).start()

            @pl.when(my_ang != p)
            def _():
                block_copy(me, p, my_row).start()


    got[me] = sent[my_ang]

    def frac_wait(step, carry):
        peer = lax.rem(my_ang + step, n_ang)
        frac_copy(peer, peer).wait()
        return carry

    lax.fori_loop(1, n_ang, frac_wait, 0)

    slots = order.shape[0] // n_row
    depth = total * size
    zs = slots * SLAB_Z
    place = iota((zs, depth), 1)
    level = iota((zs, depth), 0)
    source_ang = (place >> log2(n_row * size))
    piece_row = ((place >> log2(size)) & (n_row - 1)) * rows + (place & (rows - 1))
    half_of = ((place & (size - 1)) >> log2(ar))
    starts = jnp.zeros((zs, depth), jnp.int32)
    fraction = jnp.zeros((zs, depth), F32)
    for p in range(n_ang):
        here = source_ang == p
        spread = jnp.concatenate([frac_all[p][0:1]] * (depth // 128), axis=1)
        fraction = jnp.where(here, jnp.broadcast_to(spread, (zs, depth)), fraction)
        for k in range(slots):
            first = offsets[p, order[my_row * slots + k]]
            starts = jnp.where(here & ((level >> log2(SLAB_Z)) == k), first, starts)
    reach = piece_row - starts - (level & (SLAB_Z - 1))
    weights = jnp.where(reach == 0, 1.0 - fraction, jnp.where(reach == 1, fraction, 0.0))
    parts = []
    for h in range(halves):
        left_over = jnp.where(half_of == h, weights, 0.0)
        for _ in range(3):
            part = left_over.astype(BF16)
            left_over = left_over - part.astype(F32)
            parts.append(part)
    stacked = jnp.concatenate(parts, axis=0)

    others = got.at[pl.ds(0, total - 1)]
    pltpu.make_async_copy(others, others, recv_sem).wait()

    sums = dot(stacked, got[...].reshape(depth, 128))
    for h in range(halves):
        three = [sums[(h * 3 + s) * zs : (h * 3 + s + 1) * zs] for s in range(3)]
        vol_out[:, pl.ds(h * 128, 128)] = (three[2] + three[1] + three[0]) / math.sqrt(n_ang * angs)
    pltpu.make_async_copy(others, others, send_sem).wait()
    for copy in halo_copies:
        copy.wait_send()


def per_device(
    n_ang, n_row, dual_field, forward, sinogram, first_weight, first_bias, middle_weight,
    middle_bias, last_weight, magnify, detector_shift, row_fraction, offsets, slab_order,
):
    angs, rows, cols = dual_field.shape
    ch = first_weight.shape[2]
    operands = (
        dual_field, forward, sinogram, first_weight.transpose(0, 1, 3, 2), first_bias[None, :],
        middle_weight, middle_bias[None, :], last_weight.transpose(0, 2, 1, 3), magnify,
        detector_shift, row_fraction, offsets, slab_order,
    )
    total = n_ang * n_row
    ar = angs * rows
    out1, out2 = angs + 4, angs + 2
    narrow = cols // 128
    width = cols // n_ang
    size = width // 128 * ar
    slots = slab_order.shape[0] // n_row
    vmem = pl.BlockSpec(memory_space=pltpu.VMEM)
    dma = pltpu.SemaphoreType.DMA
    return pl.pallas_call(
        functools.partial(kernel, n_ang, n_row),
        out_shape=(
            pltpu.VMEM(dual_field.shape, BF16),
            pltpu.VMEM((slots * SLAB_Z, width), F32),
        ),
        in_specs=[pl.BlockSpec(memory_space=pltpu.HBM)] * 13,
        out_specs=(vmem, vmem),
        scratch_shapes=[pltpu.VMEM(x.shape, x.dtype) for x in operands[:8]]
        + [pltpu.SMEM(x.shape, x.dtype) for x in operands[8:]]
        + [
            pltpu.VMEM((2, 3, 3, rows, cols), BF16),
            pltpu.VMEM((64, cols), F32),
            pltpu.VMEM((3 * 64, cols), BF16),
            pltpu.VMEM((rows * 3 * out1 * ch, cols), BF16),
            pltpu.VMEM((rows * out2 * ch, cols), BF16),
            pltpu.VMEM((32, ch), F32),
            pltpu.VMEM((rows * out1 * ch, 3 * 64), BF16),
            pltpu.VMEM((out2 * ch, 3 * out1 * ch), BF16),
            pltpu.VMEM((4 * ar, rows * out2 * ch), BF16),
            pltpu.VMEM((128, 2 * narrow * 128), BF16),
            pltpu.VMEM((8, 128), F32),
            pltpu.VMEM((n_ang, 8, 128), F32),
            pltpu.VMEM((n_ang, size, 128), BF16),
            pltpu.VMEM((total, size, 128), BF16),
            dma((2, 3)),
            dma((2, 3)),
            dma((n_ang,)),
            dma((n_ang,)),
            dma(()),
            dma(()),
            dma((13,)),
        ],
        compiler_params=pltpu.CompilerParams(
            collective_id=0, has_side_effects=True, vmem_limit_bytes=65280 * 1024
        ),
        cost_estimate=pl.CostEstimate(flops=10**9, bytes_accessed=10**6, transcendentals=0),
    )(*operands)


def solution(mesh):
    sizes = dict(mesh.shape)
    split = P("ang", "row", None)
    return jax.shard_map(
        functools.partial(per_device, sizes["ang"], sizes["row"]),
        mesh=mesh,
        in_specs=(
            split, split, split, P(), P(), P(), P(), P(), P("ang"), P("ang"), P("ang"), P(), P(),
        ),
        out_specs=(split, P("row", "ang")),
        check_vma=False,
    )
```
